32 devices in a mesh: dp: 8 (over z, x), tensor: 4 (over y, core).
Axes of the slice: x: 2, y: 2, z: 4, core: 2. Of those that a mesh axis runs over, the one named last changes fastest.
Arguments:
- layer_input: float32 [8, 1024, 768], P('dp', 'tensor'), may hold values from -40 to 40
- out_cotangent: float32 [8, 1024, 768], P('dp', 'tensor'), may hold values from -6 to 6
- mix_gain: bfloat16 [768], P('dp'), may hold values from 0.099609375 to 1.8984375
- mix_shift: bfloat16 [768], P('dp'), may hold values from -4 to 4
- query_weight: bfloat16 [768, 768], P('dp', 'tensor'), may hold values from -2 to 2
- query_bias: bfloat16 [64, 12], P('dp', 'tensor'), may hold values from -3 to 3
- key_weight: bfloat16 [768, 768], P('dp', 'tensor'), may hold values from -2 to 2
- value_weight: bfloat16 [768, 768], P('dp', 'tensor'), may hold values from -0.21875 to 0.21875
- value_bias: bfloat16 [64, 12], P('dp', 'tensor'), may hold values from -0.59765625 to 0.59765625
- output_weight: bfloat16 [768, 768], P('dp', 'tensor'), may hold values from -1.75 to 1.75
- output_bias: bfloat16 [768], P('dp'), may hold values from -4 to 4
- feed_gain: bfloat16 [768], P('dp'), may hold values from 0.099609375 to 1.8984375
- feed_shift: bfloat16 [768], P('dp'), may hold values from -4 to 4
- inner_weight: bfloat16 [768, 3072], P('dp', 'tensor'), may hold values from -0.21875 to 0.21875
- inner_bias: bfloat16 [64, 48], P('dp', 'tensor'), may hold values from -3 to 3
- outer_weight: bfloat16 [768, 3072], P('dp', 'tensor'), may hold values from -0.3125 to 0.3125
- outer_bias: bfloat16 [768], P('dp'), may hold values from -4 to 4
Outputs:
- layer_output: float32 [8, 1024, 768], P('dp', 'tensor')
- input_grad: float32 [8, 1024, 768], P('dp', 'tensor')
- mix_gain_grad: float32 [768], P(('dp', 'tensor'))
- mix_shift_grad: float32 [768], P(('dp', 'tensor'))
- query_weight_grad: float32 [768, 768], P('dp', 'tensor')
- query_bias_grad: float32 [64, 12], P('dp', 'tensor')
- key_weight_grad: float32 [768, 768], P('dp', 'tensor')
- value_weight_grad: float32 [768, 768], P('dp', 'tensor')
- value_bias_grad: float32 [64, 12], P('dp', 'tensor')
- output_weight_grad: float32 [768, 768], P('dp', 'tensor')
- output_bias_grad: float32 [768], P(('dp', 'tensor'))
- feed_gain_grad: float32 [768], P(('dp', 'tensor'))
- feed_shift_grad: float32 [768], P(('dp', 'tensor'))
- inner_weight_grad: float32 [768, 3072], P('dp', 'tensor')
- inner_bias_grad: float32 [64, 48], P('dp', 'tensor')
- outer_weight_grad: float32 [768, 3072], P('dp', 'tensor')
- outer_bias_grad: float32 [768], P(('dp', 'tensor'))
The draws below stay inside these ranges and needn't reach their ends.
All inputs are finite; a program needn't handle non-finite values.
Results may differ from the reference program's by a relative error of at most 0.02.
Values may be sent and summed in bfloat16 or wider, within the bound.
A program may use at most 128 MiB of HBM per device.

```python
import math
import jax
import jax.numpy as jnp
from jax import lax

D = 768
H = 12
HD = 64
FF = 3072
FRAMES = 1024
CLIPS = 8


def clipped_normal(key, shape):
    return jnp.clip(jax.random.normal(key, shape, jnp.float32), -4.0, 4.0)


def log_spread(key, shape, lower, upper):
    return jnp.exp(jax.random.uniform(key, shape, jnp.float32, math.log(lower), math.log(upper)))


def draw_layer_input(key, part):
    entries = jnp.clip(jax.random.normal(jax.random.fold_in(key, 13), (CLIPS, FRAMES, D), jnp.float32), -3.0, 3.0)
    row_scale = log_spread(jax.random.fold_in(key, 17), (CLIPS, FRAMES, 1), 0.6, 2.5)
    column_scale = log_spread(jax.random.fold_in(key, 19), (1, 1, D), 0.6, 1.6)
    return (entries * row_scale * column_scale).astype(jnp.float32)


def projection_entries(key, salt):
    entries = clipped_normal(jax.random.fold_in(key, salt), (D, D))
    return (entries * (1.0 / math.sqrt(D))).astype(jnp.bfloat16)


def draw_query_weight(key, part):
    return projection_entries(key, 41)


def draw_key_weight(key, part):
    return projection_entries(key, 43)


def raised(drawn, rng, source, target, blocks, factor):
    def block_of(position):
        return (jnp.arange(drawn.shape[position]) // (drawn.shape[position] // blocks)).reshape((-1,) + (1,) * (drawn.ndim - 1 - position))

    one_side = jax.random.permutation(rng, blocks)[block_of(target)]
    other_side = (block_of(target) + blocks // 2) % blocks
    return jnp.where((block_of(source) == one_side) | (block_of(source) == other_side), factor * drawn, drawn)


def block_scale(stream_key, shape, pieces, low, high):
    level = 1.0
    for axis_at, blocks in pieces:
        steps = jax.random.uniform(jax.random.fold_in(jax.random.fold_in(stream_key, 6), axis_at), (blocks,), jnp.float32, low / len(pieces), high / len(pieces))
        level = level * jnp.repeat(jnp.exp(steps), shape[axis_at] // blocks).reshape((-1,) + (1,) * (len(shape) - 1 - axis_at))
    return level


def noise(key, shape, deviation, most, split=(), held_as=jnp.bfloat16):
    level = block_scale(key, shape, split, -0.22, 0.18) if split else 1.0
    values = jax.random.normal(key, shape, jnp.float32) * deviation * level
    return jnp.minimum(jnp.maximum(values, -most), most).astype(held_as)


def gaussian_with(key, shape, scale, bound, cuts, heavy, held_as=jnp.bfloat16):
    values = scale * jax.random.normal(key, shape, jnp.float32)
    if cuts:
        values = values * block_scale(key, shape, cuts, -0.22, 0.18)
    return jnp.clip(raised(values, jax.random.fold_in(key, 3), *heavy), -bound, bound).astype(held_as)


def setup_inputs(seed: int = 0) -> dict:
    splits = jax.random.split(jax.random.key(seed), 18)
    layer_input = draw_layer_input(jax.random.fold_in(splits[17], 71), 0)
    out_cotangent = gaussian_with(splits[1], (CLIPS, FRAMES, D), 1.0, 6.0, ((0, 8), (1, 4)), (0, 2, 8, 2.0), jnp.float32)
    mix_gain = jnp.clip(1.0 + 0.18 * jax.random.normal(splits[2], (D,), jnp.float32), 0.099609375, 1.8984375).astype(jnp.bfloat16)
    mix_shift = noise(splits[3], (D,), 0.8, 4.0, ((0, 8),))
    query_weight = draw_query_weight(jax.random.fold_in(splits[17], 71), 0)
    query_bias = noise(splits[5], (HD, H), 0.5, 3.0, ((0, 8), (1, 4)))
    key_weight = draw_key_weight(jax.random.fold_in(splits[17], 71), 0)
    value_weight = noise(splits[7], (D, D), D ** -0.5, 0.21875, ((0, 8), (1, 4)))
    value_bias = noise(splits[8], (HD, H), 0.1, 0.59765625, ((0, 8), (1, 4)))
    output_weight = noise(splits[9], (D, D), (D // 64) ** -0.5, 1.75, ((0, 8), (1, 4)))
    output_bias = noise(splits[10], (D,), 1.0, 4.0, ((0, 8),))
    feed_gain = jnp.clip(1.0 + 0.18 * jax.random.normal(splits[11], (D,), jnp.float32), 0.099609375, 1.8984375).astype(jnp.bfloat16)
    feed_shift = noise(splits[12], (D,), 0.8, 4.0, ((0, 8),))
    inner_weight = noise(splits[13], (D, FF), D ** -0.5, 0.21875, ((0, 8), (1, 4)))
    inner_bias = noise(splits[14], (HD, FF // HD), 0.5, 3.0, ((0, 8), (1, 4)))
    outer_weight = noise(splits[15], (D, FF), (FF // 8) ** -0.5, 0.3125, ((0, 8), (1, 4)))
    outer_bias = noise(splits[16], (D,), 1.0, 4.0, ((0, 8),))
    return dict(layer_input=layer_input, out_cotangent=out_cotangent, mix_gain=mix_gain, mix_shift=mix_shift, query_weight=query_weight, query_bias=query_bias, key_weight=key_weight, value_weight=value_weight, value_bias=value_bias, output_weight=output_weight, output_bias=output_bias, feed_gain=feed_gain, feed_shift=feed_shift, inner_weight=inner_weight, inner_bias=inner_bias, outer_weight=outer_weight, outer_bias=outer_bias)


EPS = 1e-05
ROOT_HALF = 0.7071067811865476
DENSITY_NORM = 0.3989422804014327

def layer_norm(block, gain, shift):
    row_mean = lax.optimization_barrier(jnp.mean(block, axis=-1, keepdims=True))
    centred = block - row_mean
    rstd = lax.rsqrt(lax.optimization_barrier(jnp.mean(centred * centred, axis=-1, keepdims=True)) + EPS)
    normed = centred * rstd
    lowered = (normed * gain.astype(jnp.float32) + shift.astype(jnp.float32)).astype(jnp.bfloat16)
    return (normed, rstd, lowered)

def norm_backward(gradient, normed, rstd, gain):
    scaled = gradient * gain.astype(jnp.float32)
    first = lax.optimization_barrier(jnp.mean(scaled, axis=-1, keepdims=True))
    second = lax.optimization_barrier(jnp.mean(scaled * normed, axis=-1, keepdims=True))
    return (scaled - first - normed * second) * rstd

def gelu_value(preact):
    return 0.5 * preact * (1.0 + lax.erf(preact * ROOT_HALF))

def gelu_slope(preact):
    return 0.5 * (1.0 + lax.erf(preact * ROOT_HALF)) + preact * DENSITY_NORM * jnp.exp(-0.5 * preact * preact)

def heads_of(block):
    return block.astype(jnp.float32).reshape(block.shape[0], H, HD)

def attend(queries, key_rows, values):
    score_scale = 1.0 / math.sqrt(HD)
    scores = jnp.einsum('qhd,khd->hqk', heads_of(queries), heads_of(key_rows)) * score_scale
    row_max = lax.optimization_barrier(jnp.max(scores, axis=-1, keepdims=True))
    log_total = row_max + jnp.log(lax.optimization_barrier(jnp.sum(jnp.exp(scores - row_max), axis=-1, keepdims=True)))
    prob_low = jnp.exp(scores - log_total).astype(jnp.bfloat16)
    context = jnp.einsum('hqk,khd->qhd', prob_low.astype(jnp.float32), heads_of(values))
    return (context.reshape(queries.shape[0], D).astype(jnp.bfloat16), log_total)

def attend_back(queries, key_rows, values, context_grad, log_total):
    score_scale = 1.0 / math.sqrt(HD)
    query_heads = heads_of(queries)
    key_heads = heads_of(key_rows)
    grad_heads = heads_of(context_grad)
    scores = jnp.einsum('qhd,khd->hqk', query_heads, key_heads) * score_scale
    prob_full = jnp.exp(scores - log_total)
    prob_low = prob_full.astype(jnp.bfloat16).astype(jnp.float32)
    value_grad = jnp.einsum('hqk,qhd->khd', prob_low, grad_heads)
    prob_grad = jnp.einsum('qhd,khd->hqk', grad_heads, heads_of(values))
    row_dot = lax.optimization_barrier(jnp.sum(prob_full * prob_grad, axis=-1, keepdims=True))
    score_grad = (prob_full * (prob_grad - row_dot) * score_scale).astype(jnp.bfloat16).astype(jnp.float32)
    query_grad = jnp.einsum('hqk,khd->qhd', score_grad, key_heads)
    key_low = jnp.einsum('hqk,qhd->khd', score_grad, query_heads).astype(jnp.bfloat16)
    frames = queries.shape[0]
    return (query_grad.reshape(frames, D), key_low.reshape(frames, D), value_grad.reshape(frames, D))

def matmul(left, right):
    return jnp.dot(left, right, preferred_element_type=jnp.float32)

def reference(layer_input, out_cotangent, mix_gain, mix_shift, query_weight, query_bias, key_weight, value_weight, value_bias, output_weight, output_bias, feed_gain, feed_shift, inner_weight, inner_bias, outer_weight, outer_bias):
    bias_query = query_bias.astype(jnp.float32).T.reshape(-1)
    bias_value = value_bias.astype(jnp.float32).T.reshape(-1)
    bias_inner = inner_bias.astype(jnp.float32).T.reshape(-1)

    def per_clip(totals, clip_pair):
        clip_input, clip_cot = clip_pair
        normed_one, rstd_one, lowered_one = layer_norm(clip_input, mix_gain, mix_shift)
        queries = (matmul(lowered_one, query_weight) + bias_query).astype(jnp.bfloat16)
        key_rows = matmul(lowered_one, key_weight).astype(jnp.bfloat16)
        values = (matmul(lowered_one, value_weight) + bias_value).astype(jnp.bfloat16)
        context, log_total = attend(queries, key_rows, values)
        mixed = clip_input + matmul(context, output_weight.T) + output_bias.astype(jnp.float32)
        normed_two, rstd_two, lowered_two = layer_norm(mixed, feed_gain, feed_shift)
        preact = matmul(lowered_two, inner_weight) + bias_inner
        hidden = gelu_value(preact).astype(jnp.bfloat16)
        clip_output = mixed + matmul(hidden, outer_weight.T) + outer_bias.astype(jnp.float32)
        cot_low = clip_cot.astype(jnp.bfloat16)
        preact_grad = matmul(cot_low, outer_weight) * gelu_slope(preact)
        preact_low = preact_grad.astype(jnp.bfloat16)
        outer_grad = matmul(cot_low.T, hidden)
        inner_grad = matmul(lowered_two.T, preact_low)
        norm_two_grad = matmul(preact_low, inner_weight.T)
        mixed_grad = clip_cot + norm_backward(norm_two_grad, normed_two, rstd_two, feed_gain)
        mixed_low = mixed_grad.astype(jnp.bfloat16)
        output_grad = matmul(mixed_low.T, context)
        context_grad = matmul(mixed_low, output_weight).astype(jnp.bfloat16)
        query_grad, key_low, value_grad = attend_back(queries, key_rows, values, context_grad, log_total)
        query_low = query_grad.astype(jnp.bfloat16)
        value_low = value_grad.astype(jnp.bfloat16)
        norm_one_grad = matmul(query_low, query_weight.T) + matmul(key_low, key_weight.T) + matmul(value_low, value_weight.T)
        clip_grad = mixed_grad + norm_backward(norm_one_grad, normed_one, rstd_one, mix_gain)
        terms = (lax.optimization_barrier(jnp.sum(norm_one_grad * normed_one, axis=0)), lax.optimization_barrier(jnp.sum(norm_one_grad, axis=0)), matmul(lowered_one.T, query_low), lax.optimization_barrier(jnp.sum(query_grad, axis=0)), matmul(lowered_one.T, key_low), matmul(lowered_one.T, value_low), lax.optimization_barrier(jnp.sum(value_grad, axis=0)), output_grad, lax.optimization_barrier(jnp.sum(mixed_grad, axis=0)), lax.optimization_barrier(jnp.sum(norm_two_grad * normed_two, axis=0)), lax.optimization_barrier(jnp.sum(norm_two_grad, axis=0)), inner_grad, lax.optimization_barrier(jnp.sum(preact_grad, axis=0)), outer_grad, lax.optimization_barrier(jnp.sum(clip_cot, axis=0)))
        updated = tuple((total + term for total, term in zip(totals, terms)))
        return (updated, (clip_output, clip_grad))
    zeros_d = jnp.zeros((D,), jnp.float32)
    zeros_square = jnp.zeros((D, D), jnp.float32)
    zeros_wide = jnp.zeros((D, FF), jnp.float32)
    initial = (zeros_d, zeros_d, zeros_square, zeros_d, zeros_square, zeros_square, zeros_d, zeros_square, zeros_d, zeros_d, zeros_d, zeros_wide, jnp.zeros((FF,), jnp.float32), zeros_wide, zeros_d)
    totals, (layer_output, input_grad) = lax.scan(per_clip, initial, (layer_input, out_cotangent))
    mix_gain_grad, mix_shift_grad, query_weight_grad, query_bias_sum, key_weight_grad, value_weight_grad, value_bias_sum, output_weight_grad, output_bias_grad, feed_gain_grad, feed_shift_grad, inner_weight_grad, inner_bias_sum, outer_weight_grad, outer_bias_grad = totals
    query_bias_grad = query_bias_sum.reshape(H, HD).T
    value_bias_grad = value_bias_sum.reshape(H, HD).T
    inner_bias_grad = inner_bias_sum.reshape(FF // HD, HD).T
    return (layer_output, input_grad, mix_gain_grad, mix_shift_grad, query_weight_grad, query_bias_grad, key_weight_grad, value_weight_grad, value_bias_grad, output_weight_grad, output_bias_grad, feed_gain_grad, feed_shift_grad, inner_weight_grad, inner_bias_grad, outer_weight_grad, outer_bias_grad)
```

```python
import functools
import math

import jax
import jax.numpy as jnp
from jax import lax
from jax.experimental import pallas as pl
from jax.experimental.pallas import tpu as pltpu
from jax.sharding import PartitionSpec as P

HD = 64
EPS = 1e-05
ROOT_HALF = 0.7071067811865476
DENSITY_NORM = 0.3989422804014327
MESH = pl.DeviceIdType.MESH
CHUNK = 64
VROWS = 8
F32 = jnp.float32
BF16 = jnp.bfloat16


def gelu_value(preact):
    return 0.5 * preact * (1.0 + lax.erf(preact * ROOT_HALF))


def gelu_slope(preact):
    return 0.5 * (1.0 + lax.erf(preact * ROOT_HALF)) + preact * DENSITY_NORM * jnp.exp(
        -0.5 * preact * preact
    )


def matmul(left, right):
    return jnp.dot(left, right, preferred_element_type=F32)


def matmul_nt(left, right):
    return lax.dot_general(left, right, (((1,), (1,)), ((), ())), preferred_element_type=F32)


def split_heads(block):
    return block.reshape(block.shape[0], block.shape[1] // HD, HD)


def places():
    d = lax.axis_index("dp")
    t = lax.axis_index("tensor")
    sib = t + 1 - 2 * lax.rem(t, 2)
    opp = lax.rem(t + 2, 4)
    diag = lax.rem(sib + 2, 4)
    return d, t, sib, opp, diag


def greet(dp, tensor_peers):
    d, t = lax.axis_index("dp"), lax.axis_index("tensor")
    barrier = pltpu.get_barrier_semaphore()
    for peer in tensor_peers:
        pl.semaphore_signal(barrier, inc=1, device_id=(d, peer), device_id_type=MESH)

    def signal(k, carry):
        pl.semaphore_signal(
            barrier, inc=1, device_id=(lax.rem(d + k, dp), t), device_id_type=MESH
        )
        return carry

    if dp > 1:
        lax.fori_loop(1, dp, signal, 0)
    pl.semaphore_wait(barrier, len(tensor_peers) + dp - 1)


def normed_rows(block):
    row_mean = jnp.mean(block, axis=-1, keepdims=True)
    centred = block - row_mean
    rstd = lax.rsqrt(jnp.mean(centred * centred, axis=-1, keepdims=True) + EPS)
    return centred * rstd, rstd


def norm_back(gradient, normed, rstd, gain):
    scaled = gradient * gain
    first = jnp.mean(scaled, axis=-1, keepdims=True)
    second = jnp.mean(scaled * normed, axis=-1, keepdims=True)
    return (scaled - first - normed * second) * rstd


def rows_of(c):
    return pl.ds(c * CHUNK, CHUNK)


class Gather:
    def __init__(self, buf, send, recv):
        self.buf, self.send, self.recv = buf, send, recv
        self.chunks = buf.shape[1] // CHUNK

    def copy(self, slot, kind, c, peer):
        d = lax.axis_index("dp")
        ref = self.buf.at[slot, rows_of(c)]
        return pltpu.make_async_remote_copy(
            src_ref=ref,
            dst_ref=ref,
            send_sem=self.send.at[kind, c],
            recv_sem=self.recv.at[kind, c],
            device_id=(d, peer),
            device_id_type=MESH,
        )

    def start(self, c):
        _, t, sib, opp, _ = places()
        self.copy(t, 1, c, opp).start()
        self.copy(t, 0, c, sib).start()

    def forward(self, c):
        _, t, sib, opp, _ = places()
        self.copy(opp, 1, c, opp).wait_recv()
        self.copy(opp, 2, c, sib).start()

    def finish(self):
        _, t, sib, opp, diag = places()
        for c in range(self.chunks):
            self.copy(sib, 0, c, sib).wait_recv()
            self.copy(diag, 2, c, sib).wait_recv()
        for c in range(self.chunks):
            self.copy(t, 0, c, sib).wait_send()
            self.copy(t, 1, c, opp).wait_send()
            self.copy(opp, 2, c, sib).wait_send()


class Scatter:
    def __init__(self, part, near, total, far, send, recv):
        self.part, self.near, self.total, self.far = part, near, total, far
        self.send, self.recv = send, recv
        self.chunks = part.shape[1] // CHUNK

    def copy(self, src, dst, kind, c, peer):
        d = lax.axis_index("dp")
        return pltpu.make_async_remote_copy(
            src_ref=src,
            dst_ref=dst,
            send_sem=self.send.at[kind, c],
            recv_sem=self.recv.at[kind, c],
            device_id=(d, peer),
            device_id_type=MESH,
        )

    def to_sibling(self, kind, c):
        _, _, sib, _, diag = places()
        block = sib if kind == 0 else diag
        return self.copy(
            self.part.at[block, rows_of(c)], self.near.at[kind, rows_of(c)], kind, c, sib
        )

    def across(self, c):
        _, _, _, opp, _ = places()
        return self.copy(self.total.at[rows_of(c)], self.far.at[rows_of(c)], 2, c, opp)

    def start(self):
        for c in range(self.chunks):
            self.to_sibling(1, c).start()
        for c in range(self.chunks):
            self.to_sibling(0, c).start()

    def middle(self, c):
        _, _, _, opp, _ = places()
        self.to_sibling(1, c).wait_recv()
        rows = rows_of(c)
        self.total[rows, :] = (
            self.part[opp, rows, :].astype(F32) + self.near[1, rows, :].astype(F32)
        ).astype(BF16)
        self.across(c).start()

    def result(self, c):
        _, t, _, _, _ = places()
        self.to_sibling(0, c).wait_recv()
        self.across(c).wait_recv()
        rows = rows_of(c)
        return (
            self.part[t, rows, :].astype(F32)
            + self.near[0, rows, :].astype(F32)
            + self.far[rows, :].astype(F32)
        )

    def finish(self):
        for c in range(self.chunks):
            self.to_sibling(0, c).wait_send()
            self.to_sibling(1, c).wait_send()
            self.across(c).wait_send()


def scatter_scratch(rows, width):
    return [
        pltpu.VMEM((2, rows, width), BF16),
        pltpu.VMEM((rows, width), BF16),
        pltpu.VMEM((rows, width), BF16),
        pltpu.SemaphoreType.DMA((3, rows // CHUNK)),
        pltpu.SemaphoreType.DMA((3, rows // CHUNK)),
    ]


def gather_scratch(rows):
    return [
        pltpu.SemaphoreType.DMA((3, rows // CHUNK)),
        pltpu.SemaphoreType.DMA((3, rows // CHUNK)),
    ]


def dp_copy(dp, k, src, dst, send, recv):
    d, t = lax.axis_index("dp"), lax.axis_index("tensor")
    return pltpu.make_async_remote_copy(
        src_ref=src,
        dst_ref=dst,
        send_sem=send.at[k],
        recv_sem=recv.at[k],
        device_id=(lax.rem(d + k, dp), t),
        device_id_type=MESH,
    )


def each_peer(dp, body):
    def step(k, carry):
        body(k)
        return carry

    lax.fori_loop(1, dp, step, 0)


def first_kernel(
    dp, x_ref, cot_ref, small_ref, pack_ref,
    gathered_ref, vec_ref, low_ref, cot_all_ref,
    small_buf, s_send, s_recv, w_send, w_recv, own_sem, l_send, l_recv, c_send, c_recv,
):
    d, t, sib, opp, diag = places()
    own = pltpu.make_async_copy(pack_ref, gathered_ref.at[d], own_sem)
    own.start()
    small_buf[d] = small_ref[...]
    greet(dp, (sib, opp))

    def small_copy(k):
        return dp_copy(dp, k, small_buf.at[d], small_buf.at[d], s_send, s_recv)

    def pack_copy(k):
        return dp_copy(dp, k, pack_ref, gathered_ref.at[d], w_send, w_recv)

    each_peer(dp, lambda k: small_copy(k).start())
    each_peer(dp, lambda k: pack_copy(k).start())
    low = Gather(low_ref, l_send, l_recv)
    cot = Gather(cot_all_ref, c_send, c_recv)
    each_peer(dp, lambda k: small_copy(k).wait_recv())
    vec_ref[...] = jnp.sum(small_buf[...], axis=0)
    gain, shift = vec_ref[0:1, :], vec_ref[1:2, :]
    for c in range(low.chunks):
        normed, _ = normed_rows(x_ref[rows_of(c), :])
        low_ref[t, rows_of(c), :] = (normed * gain + shift).astype(BF16)
        low.start(c)
    for c in range(cot.chunks):
        cot_all_ref[t, rows_of(c), :] = cot_ref[rows_of(c), :].astype(BF16)
        cot.start(c)
    for c in range(low.chunks):
        low.forward(c)
    for c in range(cot.chunks):
        cot.forward(c)
    low.finish()
    cot.finish()
    each_peer(dp, lambda k: small_copy(k).wait_send())
    each_peer(dp, lambda k: pack_copy(k).wait())
    own.wait()


def second_kernel(
    part_ref, x_ref, vec_ref,
    mixed_ref, low_ref,
    near, total, far, r_send, r_recv, l_send, l_recv,
):
    d, t, sib, opp, diag = places()
    greet(1, (sib, opp))
    scat = Scatter(part_ref, near, total, far, r_send, r_recv)
    low = Gather(low_ref, l_send, l_recv)
    scat.start()
    for c in range(scat.chunks):
        scat.middle(c)
    bias, gain, shift = vec_ref[2:3, :], vec_ref[3:4, :], vec_ref[4:5, :]
    for c in range(scat.chunks):
        mixed = x_ref[rows_of(c), :] + scat.result(c) + bias
        mixed_ref[rows_of(c), :] = mixed
        normed, _ = normed_rows(mixed)
        low_ref[t, rows_of(c), :] = (normed * gain + shift).astype(BF16)
        low.start(c)
    for c in range(low.chunks):
        low.forward(c)
    low.finish()
    scat.finish()


def third_kernel(
    npart_ref, fpart_ref, mixed_ref, cot_ref, vec_ref,
    grad_ref, all_ref, out_ref, sums_ref,
    n_near, n_total, n_far, n_send, n_recv,
    f_near, f_total, f_far, f_send, f_recv,
    g_send, g_recv,
):
    d, t, sib, opp, diag = places()
    greet(1, (sib, opp))
    first = Scatter(npart_ref, n_near, n_total, n_far, n_send, n_recv)
    feed = Scatter(fpart_ref, f_near, f_total, f_far, f_send, f_recv)
    gather = Gather(all_ref, g_send, g_recv)
    first.start()
    for c in range(first.chunks):
        first.middle(c)
    feed.start()
    gain = vec_ref[3:4, :]
    sums = [jnp.zeros_like(gain) for _ in range(4)]
    for c in range(first.chunks):
        gradient = first.result(c)
        cot = cot_ref[rows_of(c), :]
        normed, rstd = normed_rows(mixed_ref[rows_of(c), :])
        mixed_grad = cot + norm_back(gradient, normed, rstd, gain)
        grad_ref[rows_of(c), :] = mixed_grad
        all_ref[t, rows_of(c), :] = mixed_grad.astype(BF16)
        gather.start(c)
        terms = (mixed_grad, gradient * normed, gradient, cot)
        sums = [s + jnp.sum(v, axis=0, keepdims=True) for s, v in zip(sums, terms)]
    zero = jnp.zeros_like(gain)
    sums_ref[...] = jnp.concatenate([zero, zero] + sums + [zero, zero], axis=0)
    for c in range(feed.chunks):
        feed.middle(c)
    for c in range(gather.chunks):
        gather.forward(c)
    bias = vec_ref[5:6, :]
    for c in range(feed.chunks):
        out_ref[rows_of(c), :] = mixed_ref[rows_of(c), :] + feed.result(c) + bias
    gather.finish()
    first.finish()
    feed.finish()


def fourth_kernel(
    dp, part_ref, x_ref, mixed_grad_ref, vec_ref, sums_ref, wgrad_ref,
    input_grad_ref, wout_ref, vout_ref,
    near, total, far, r_send, r_recv,
    landed, w_send, w_recv, group, t_send, t_recv, whole, v_send, v_recv,
):
    d, t, sib, opp, diag = places()
    greet(dp, (sib, opp, diag))
    scat = Scatter(part_ref, near, total, far, r_send, r_recv)
    scat.start()

    def weight_copy(k):
        return dp_copy(
            dp, k, wgrad_ref.at[lax.rem(d + k, dp)], landed.at[d], w_send, w_recv
        )

    each_peer(dp, lambda k: weight_copy(k).start())
    for c in range(scat.chunks):
        scat.middle(c)
    gain = vec_ref[0:1, :]
    sums = [jnp.zeros_like(gain) for _ in range(2)]
    for c in range(scat.chunks):
        gradient = scat.result(c)
        normed, rstd = normed_rows(x_ref[rows_of(c), :])
        input_grad_ref[rows_of(c), :] = mixed_grad_ref[rows_of(c), :] + norm_back(
            gradient, normed, rstd, gain
        )
        terms = (gradient * normed, gradient)
        sums = [s + jnp.sum(v, axis=0, keepdims=True) for s, v in zip(sums, terms)]
    mine = sums_ref[...] + jnp.concatenate(
        sums + [jnp.zeros((VROWS - 2, gain.shape[1]), F32)], axis=0
    )
    group[t] = mine
    tensor_copies = [
        pltpu.make_async_remote_copy(
            src_ref=group.at[t],
            dst_ref=group.at[t],
            send_sem=t_send.at[i],
            recv_sem=t_recv.at[i],
            device_id=(d, peer),
            device_id_type=MESH,
        )
        for i, peer in enumerate((sib, opp, diag))
    ]
    for copy in tensor_copies:
        copy.start()
    for copy in tensor_copies:
        copy.wait()
    over_group = jnp.sum(group[...], axis=0)
    row = lax.broadcasted_iota(jnp.int32, mine.shape, 0)
    whole[d] = jnp.where(row < 6, over_group, mine)

    def vector_copy(k):
        return dp_copy(dp, k, whole.at[d], whole.at[d], v_send, v_recv)

    each_peer(dp, lambda k: vector_copy(k).start())
    landed[d] = wgrad_ref[d]
    each_peer(dp, lambda k: weight_copy(k).wait())
    acc = landed[0].astype(F32)
    for k in range(1, dp):
        acc = acc + landed[k].astype(F32)
    wout_ref[...] = acc
    each_peer(dp, lambda k: vector_copy(k).wait())
    vout_ref[...] = jnp.sum(whole[...], axis=0)
    scat.finish()


VM = pl.BlockSpec(memory_space=pltpu.VMEM)
ANY = pl.BlockSpec(memory_space=pl.ANY)


def comm_call(kernel, ident, in_specs, outs, out_specs, scratch, flops=20_000_000_000):
    return pl.pallas_call(
        kernel,
        out_shape=tuple(jax.ShapeDtypeStruct(s, dt) for s, dt in outs),
        in_specs=in_specs,
        out_specs=tuple(out_specs),
        scratch_shapes=scratch,
        cost_estimate=pl.CostEstimate(flops=flops, bytes_accessed=4_000_000, transcendentals=0),
        compiler_params=pltpu.CompilerParams(
            collective_id=ident, has_side_effects=True, vmem_limit_bytes=36 * 1024 * 1024
        ),
    )


def token_kernel(a_ref, b_ref, o_ref):
    o_ref[...] = lax.dot_general(
        a_ref[...], b_ref[...], (((0,), (0,)), ((), ())), preferred_element_type=F32
    ).astype(o_ref.dtype)


def token_product(left, right):
    tokens, m = left.shape
    n = right.shape[1]
    tile = 256
    return pl.pallas_call(
        token_kernel,
        grid=(m // tile,),
        out_shape=jax.ShapeDtypeStruct((m, n), BF16),
        in_specs=[
            pl.BlockSpec((tokens, tile), lambda i: (0, i)),
            pl.BlockSpec((tokens, n), lambda i: (0, 0)),
        ],
        out_specs=pl.BlockSpec((tile, n), lambda i: (i, 0)),
        cost_estimate=pl.CostEstimate(
            flops=2 * tokens * m * n, bytes_accessed=2 * (tokens * (m + n) + m * n), transcendentals=0
        ),
        compiler_params=pltpu.CompilerParams(vmem_limit_bytes=24 * 1024 * 1024),
    )(left, right)


def attend(operands):
    queries, key_rows, values = operands
    score_scale = 1.0 / math.sqrt(HD)
    scores = (
        jnp.einsum(
            "qhd,khd->hqk",
            split_heads(queries),
            split_heads(key_rows),
            preferred_element_type=jnp.float32,
        )
        * score_scale
    )
    row_max = jnp.max(scores, axis=-1, keepdims=True)
    log_total = row_max + jnp.log(jnp.sum(jnp.exp(scores - row_max), axis=-1, keepdims=True))
    prob_low = jnp.exp(scores - log_total).astype(jnp.bfloat16)
    context = jnp.einsum(
        "hqk,khd->qhd", prob_low, split_heads(values), preferred_element_type=jnp.float32
    )
    return (context.reshape(queries.shape).astype(jnp.bfloat16), log_total)


def attend_back(operands):
    queries, key_rows, values, context_grad, log_total = operands
    score_scale = 1.0 / math.sqrt(HD)
    query_heads = split_heads(queries)
    key_heads = split_heads(key_rows)
    grad_heads = split_heads(context_grad)
    scores = (
        jnp.einsum("qhd,khd->hqk", query_heads, key_heads, preferred_element_type=jnp.float32)
        * score_scale
    )
    prob_full = jnp.exp(scores - log_total)
    prob_low = prob_full.astype(jnp.bfloat16)
    value_grad = jnp.einsum(
        "hqk,qhd->khd", prob_low, grad_heads, preferred_element_type=jnp.float32
    )
    prob_grad = jnp.einsum(
        "qhd,khd->hqk", grad_heads, split_heads(values), preferred_element_type=jnp.float32
    )
    row_dot = jnp.sum(prob_full * prob_grad, axis=-1, keepdims=True)
    score_grad = (prob_full * (prob_grad - row_dot) * score_scale).astype(jnp.bfloat16)
    query_grad = jnp.einsum(
        "hqk,khd->qhd", score_grad, key_heads, preferred_element_type=jnp.float32
    )
    key_low = jnp.einsum(
        "hqk,qhd->khd", score_grad, query_heads, preferred_element_type=jnp.float32
    ).astype(jnp.bfloat16)
    return (
        query_grad.reshape(queries.shape),
        key_low.reshape(queries.shape),
        value_grad.reshape(queries.shape),
    )


def on_device(
    dp,
    layer_input,
    out_cotangent,
    mix_gain,
    mix_shift,
    query_weight,
    query_bias,
    key_weight,
    value_weight,
    value_bias,
    output_weight,
    output_bias,
    feed_gain,
    feed_shift,
    inner_weight,
    inner_bias,
    outer_weight,
    outer_bias,
):
    d = lax.axis_index("dp")
    t = lax.axis_index("tensor")
    clips, share, feats = layer_input.shape
    rows = clips * share
    frames = share * 4
    width = query_weight.shape[1]
    shard = query_weight.shape[0]
    hidden_units = inner_weight.shape[1]

    inner_full = lax.all_gather(inner_weight, "dp", axis=0, tiled=True)
    outer_full = lax.all_gather(outer_weight, "dp", axis=0, tiled=True)

    def placed_bias(bias):
        full = jnp.zeros((HD, bias.shape[1]), F32)
        full = lax.dynamic_update_slice(full, bias.astype(F32), (d * bias.shape[0], 0))
        return full.T.reshape(-1)

    vectors = jnp.stack([mix_gain, mix_shift, output_bias, feed_gain, feed_shift, outer_bias])
    upper = lax.dynamic_update_slice(
        jnp.zeros((6, feats), F32), vectors.astype(F32), (0, d * vectors.shape[1])
    )
    none = jnp.zeros((width,), F32)
    head_row = jnp.concatenate([placed_bias(query_bias), none, placed_bias(value_bias), none])
    small = jnp.concatenate([upper, head_row[None], placed_bias(inner_bias)[None]], axis=0)
    pack = jnp.concatenate([query_weight, key_weight, value_weight, output_weight], axis=1)

    x = layer_input.reshape(rows, feats)
    cot = out_cotangent.reshape(rows, feats)
    block = (4, rows, feats)

    def to_tokens(gathered):
        return (
            gathered.reshape(4, clips, share, feats)
            .transpose(1, 0, 2, 3)
            .reshape(clips * frames, feats)
        )

    def to_blocks(tokens):
        return (
            tokens.astype(BF16)
            .reshape(clips, 4, share, feats)
            .transpose(1, 0, 2, 3)
            .reshape(block)
        )

    gathered_pack, vec, low_one, cot_all = comm_call(
        functools.partial(first_kernel, dp),
        1,
        [VM, VM, VM, ANY],
        [((dp,) + pack.shape, BF16), ((VROWS, feats), F32), (block, BF16), (block, BF16)],
        [ANY, VM, VM, VM],
        [
            pltpu.VMEM((dp, VROWS, feats), F32),
            pltpu.SemaphoreType.DMA((dp,)),
            pltpu.SemaphoreType.DMA((dp,)),
            pltpu.SemaphoreType.DMA((dp,)),
            pltpu.SemaphoreType.DMA((dp,)),
            pltpu.SemaphoreType.DMA,
        ]
        + gather_scratch(rows)
        + gather_scratch(rows),
    )(x, cot, small, pack)
    flat_one = to_tokens(low_one)
    cot_tokens = to_tokens(cot_all)
    attn_weights = gathered_pack.reshape(feats, 4 * width)
    qkv_full = attn_weights[:, : 3 * width]
    output_full = attn_weights[:, 3 * width :]
    qkv = (matmul(flat_one, qkv_full) + vec[6, : 3 * width]).astype(BF16)
    clip_qkv = qkv.reshape(clips, frames, 3 * width)
    clip_queries = clip_qkv[:, :, :width]
    clip_keys = clip_qkv[:, :, width : 2 * width]
    clip_values = clip_qkv[:, :, 2 * width :]
    context, log_total = lax.map(attend, (clip_queries, clip_keys, clip_values))
    flat_context = context.reshape(clips * frames, width)
    attn_part = to_blocks(matmul_nt(flat_context, output_full))

    mixed, low_two = comm_call(
        second_kernel,
        2,
        [VM, VM, VM],
        [((rows, feats), F32), (block, BF16)],
        [VM, VM],
        scatter_scratch(rows, feats) + gather_scratch(rows),
    )(attn_part, x, vec)
    flat_two = to_tokens(low_two)
    preact = matmul(flat_two, inner_full) + vec[7, :hidden_units]
    hidden = gelu_value(preact).astype(BF16)
    preact_grad = matmul(cot_tokens, outer_full) * gelu_slope(preact)
    preact_low = preact_grad.astype(BF16)
    inner_bias_sum = jnp.sum(preact_grad, axis=0)
    norm_two_part = to_blocks(matmul_nt(preact_low, inner_full))
    feed_part = to_blocks(matmul_nt(hidden, outer_full))

    outer_part = token_product(cot_tokens, hidden)
    inner_part = token_product(flat_two, preact_low)
    inner_weight_grad = lax.psum_scatter(inner_part, "dp", scatter_dimension=0, tiled=True)
    outer_weight_grad = lax.psum_scatter(outer_part, "dp", scatter_dimension=0, tiled=True)

    mixed_grad, mixed_all, layer_output, sums = comm_call(
        third_kernel,
        3,
        [VM] * 5,
        [((rows, feats), F32), (block, BF16), ((rows, feats), F32), ((VROWS, feats), F32)],
        [VM] * 4,
        scatter_scratch(rows, feats) + scatter_scratch(rows, feats) + gather_scratch(rows),
    )(norm_two_part, feed_part, mixed, cot, vec)
    mixed_tokens = to_tokens(mixed_all)
    output_part = token_product(mixed_tokens, flat_context)
    context_grad = matmul(mixed_tokens, output_full).astype(BF16).reshape(clips, frames, width)
    query_grad, key_low, value_grad = lax.map(
        attend_back, (clip_queries, clip_keys, clip_values, context_grad, log_total)
    )
    query_grad = query_grad.reshape(clips * frames, width)
    key_low = key_low.reshape(clips * frames, width)
    value_grad = value_grad.reshape(clips * frames, width)
    low_grads = jnp.concatenate(
        [query_grad.astype(BF16), key_low, value_grad.astype(BF16)], axis=1
    )
    norm_one_part = to_blocks(matmul_nt(low_grads, qkv_full))
    attn_wpart = jnp.concatenate([token_product(flat_one, low_grads), output_part], axis=1)
    bias_row = jnp.concatenate(
        [jnp.sum(query_grad, axis=0), none, jnp.sum(value_grad, axis=0), none]
    )
    sums = sums + jnp.concatenate(
        [jnp.zeros((VROWS - 2, feats), F32), bias_row[None], inner_bias_sum[None]], axis=0
    )

    input_grad, attn_grads, vector_sums = comm_call(
        functools.partial(fourth_kernel, dp),
        4,
        [VM] * 6,
        [((rows, feats), F32), ((shard, 4 * width), F32), ((VROWS, feats), F32)],
        [VM] * 3,
        scatter_scratch(rows, feats)
        + [
            pltpu.VMEM((dp, shard, 4 * width), BF16),
            pltpu.SemaphoreType.DMA((dp,)),
            pltpu.SemaphoreType.DMA((dp,)),
            pltpu.VMEM((4, VROWS, feats), F32),
            pltpu.SemaphoreType.DMA((3,)),
            pltpu.SemaphoreType.DMA((3,)),
            pltpu.VMEM((dp, VROWS, feats), F32),
            pltpu.SemaphoreType.DMA((dp,)),
            pltpu.SemaphoreType.DMA((dp,)),
        ],
    )(norm_one_part, x, mixed_grad, vec, sums, attn_wpart.reshape(dp, shard, 4 * width))

    piece = feats // (4 * dp)
    mine = lax.dynamic_slice(vector_sums, (0, (d * 4 + t) * piece), (VROWS, piece))

    def bias_share(vector, like):
        table = vector.reshape(-1, HD).T
        return lax.dynamic_slice(table, (d * like.shape[0], 0), like.shape)

    return (
        layer_output.reshape(layer_input.shape),
        input_grad.reshape(layer_input.shape),
        mine[0],
        mine[1],
        attn_grads[:, :width],
        bias_share(vector_sums[6, :width], query_bias),
        attn_grads[:, width : 2 * width],
        attn_grads[:, 2 * width : 3 * width],
        bias_share(vector_sums[6, 2 * width : 3 * width], value_bias),
        attn_grads[:, 3 * width :],
        mine[2],
        mine[3],
        mine[4],
        inner_weight_grad.astype(F32),
        bias_share(vector_sums[7, :hidden_units], inner_bias),
        outer_weight_grad.astype(F32),
        mine[5],
    )


def solution(mesh):
    placed = (
        P("dp", "tensor", None),
        P("dp", "tensor", None),
        P("dp"),
        P("dp"),
        P("dp", "tensor"),
        P("dp", "tensor"),
        P("dp", "tensor"),
        P("dp", "tensor"),
        P("dp", "tensor"),
        P("dp", "tensor"),
        P("dp"),
        P("dp"),
        P("dp"),
        P("dp", "tensor"),
        P("dp", "tensor"),
        P("dp", "tensor"),
        P("dp"),
    )
    return jax.shard_map(
        functools.partial(on_device, mesh.shape["dp"]),
        mesh=mesh,
        in_specs=placed,
        out_specs=(
            P("dp", "tensor", None),
            P("dp", "tensor", None),
            P(("dp", "tensor")),
            P(("dp", "tensor")),
            P("dp", "tensor"),
            P("dp", "tensor"),
            P("dp", "tensor"),
            P("dp", "tensor"),
            P("dp", "tensor"),
            P("dp", "tensor"),
            P(("dp", "tensor")),
            P(("dp", "tensor")),
            P(("dp", "tensor")),
            P("dp", "tensor"),
            P("dp", "tensor"),
            P("dp", "tensor"),
            P(("dp", "tensor")),
        ),
        check_vma=False,
    )
```

```python
import functools
import math

import jax
import jax.numpy as jnp
from jax import lax
from jax.experimental import pallas as pl
from jax.experimental.pallas import tpu as pltpu
from jax.sharding import PartitionSpec as P

HD = 64
EPS = 1e-05
ROOT_HALF = 0.7071067811865476
DENSITY_NORM = 0.3989422804014327
MESH = pl.DeviceIdType.MESH
CHUNK = 64
VROWS = 8
F32 = jnp.float32
BF16 = jnp.bfloat16


def gelu_value(preact):
    return 0.5 * preact * (1.0 + lax.erf(preact * ROOT_HALF))


def gelu_slope(preact):
    return 0.5 * (1.0 + lax.erf(preact * ROOT_HALF)) + preact * DENSITY_NORM * jnp.exp(
        -0.5 * preact * preact
    )


def matmul(left, right):
    return jnp.dot(left, right, preferred_element_type=F32)


def matmul_nt(left, right):
    return lax.dot_general(left, right, (((1,), (1,)), ((), ())), preferred_element_type=F32)


def split_heads(block):
    return block.reshape(block.shape[0], block.shape[1] // HD, HD)


def places():
    d = lax.axis_index("dp")
    t = lax.axis_index("tensor")
    sib = t + 1 - 2 * lax.rem(t, 2)
    opp = lax.rem(t + 2, 4)
    diag = lax.rem(sib + 2, 4)
    return d, t, sib, opp, diag


def greet(dp, tensor_peers):
    d, t = lax.axis_index("dp"), lax.axis_index("tensor")
    barrier = pltpu.get_barrier_semaphore()
    for peer in tensor_peers:
        pl.semaphore_signal(barrier, inc=1, device_id=(d, peer), device_id_type=MESH)

    def signal(k):
        pl.semaphore_signal(
            barrier, inc=1, device_id=(lax.rem(d + k, dp), t), device_id_type=MESH
        )

    each_peer(dp, signal)
    pl.semaphore_wait(barrier, len(tensor_peers) + dp - 1)


def normed_rows(block):
    row_mean = jnp.mean(block, axis=-1, keepdims=True)
    centred = block - row_mean
    rstd = lax.rsqrt(jnp.mean(centred * centred, axis=-1, keepdims=True) + EPS)
    return centred * rstd, rstd


def norm_back(gradient, normed, rstd, gain):
    scaled = gradient * gain
    first = jnp.mean(scaled, axis=-1, keepdims=True)
    second = jnp.mean(scaled * normed, axis=-1, keepdims=True)
    return (scaled - first - normed * second) * rstd


def rows_of(c):
    return pl.ds(c * CHUNK, CHUNK)


class Gather:
    def __init__(self, buf, send, recv):
        self.buf, self.send, self.recv = buf, send, recv
        self.chunks = buf.shape[1] // CHUNK

    def copy(self, slot, kind, c, peer):
        d = lax.axis_index("dp")
        ref = self.buf.at[slot, rows_of(c)]
        return pltpu.make_async_remote_copy(
            src_ref=ref,
            dst_ref=ref,
            send_sem=self.send.at[kind, c],
            recv_sem=self.recv.at[kind, c],
            device_id=(d, peer),
            device_id_type=MESH,
        )

    def start(self, c):
        _, t, sib, opp, _ = places()
        self.copy(t, 1, c, opp).start()
        self.copy(t, 0, c, sib).start()

    def forward(self, c):
        _, t, sib, opp, _ = places()
        self.copy(opp, 1, c, opp).wait_recv()
        self.copy(opp, 2, c, sib).start()

    def finish(self):
        _, t, sib, opp, diag = places()
        for c in range(self.chunks):
            self.copy(sib, 0, c, sib).wait_recv()
            self.copy(diag, 2, c, sib).wait_recv()
        for c in range(self.chunks):
            self.copy(t, 0, c, sib).wait_send()
            self.copy(t, 1, c, opp).wait_send()
            self.copy(opp, 2, c, sib).wait_send()


class Scatter:
    def __init__(self, part, near, total, far, send, recv):
        self.part, self.near, self.total, self.far = part, near, total, far
        self.send, self.recv = send, recv
        self.chunks = part.shape[1] // CHUNK

    def copy(self, src, dst, kind, c, peer):
        d = lax.axis_index("dp")
        return pltpu.make_async_remote_copy(
            src_ref=src,
            dst_ref=dst,
            send_sem=self.send.at[kind, c],
            recv_sem=self.recv.at[kind, c],
            device_id=(d, peer),
            device_id_type=MESH,
        )

    def to_sibling(self, kind, c):
        _, _, sib, _, diag = places()
        block = sib if kind == 0 else diag
        return self.copy(
            self.part.at[block, rows_of(c)], self.near.at[kind, rows_of(c)], kind, c, sib
        )

    def across(self, c):
        _, _, _, opp, _ = places()
        return self.copy(self.total.at[rows_of(c)], self.far.at[rows_of(c)], 2, c, opp)

    def start(self):
        for c in range(self.chunks):
            self.to_sibling(1, c).start()
        for c in range(self.chunks):
            self.to_sibling(0, c).start()

    def middle(self, c):
        _, _, _, opp, _ = places()
        self.to_sibling(1, c).wait_recv()
        rows = rows_of(c)
        self.total[rows, :] = (
            self.part[opp, rows, :].astype(F32) + self.near[1, rows, :].astype(F32)
        ).astype(BF16)
        self.across(c).start()

    def result(self, c):
        _, t, _, _, _ = places()
        self.to_sibling(0, c).wait_recv()
        self.across(c).wait_recv()
        rows = rows_of(c)
        return (
            self.part[t, rows, :].astype(F32)
            + self.near[0, rows, :].astype(F32)
            + self.far[rows, :].astype(F32)
        )

    def finish(self):
        for c in range(self.chunks):
            self.to_sibling(0, c).wait_send()
            self.to_sibling(1, c).wait_send()
            self.across(c).wait_send()


def scatter_scratch(rows, width):
    return [
        pltpu.VMEM((2, rows, width), BF16),
        pltpu.VMEM((rows, width), BF16),
        pltpu.VMEM((rows, width), BF16),
        pltpu.SemaphoreType.DMA((3, rows // CHUNK)),
        pltpu.SemaphoreType.DMA((3, rows // CHUNK)),
    ]


def gather_scratch(rows):
    return [
        pltpu.SemaphoreType.DMA((3, rows // CHUNK)),
        pltpu.SemaphoreType.DMA((3, rows // CHUNK)),
    ]


def dp_copy(dp, k, src, dst, send, recv):
    d, t = lax.axis_index("dp"), lax.axis_index("tensor")
    return pltpu.make_async_remote_copy(
        src_ref=src,
        dst_ref=dst,
        send_sem=send.at[k],
        recv_sem=recv.at[k],
        device_id=(lax.rem(d + k, dp), t),
        device_id_type=MESH,
    )


def each_peer(dp, body):
    def step(k, carry):
        body(k)
        return carry

    lax.fori_loop(1, dp, step, 0)


def pair_copy(src, dst, sem_pair, index, peer):
    t = lax.axis_index("tensor")
    return pltpu.make_async_remote_copy(
        src_ref=src,
        dst_ref=dst,
        send_sem=sem_pair[0].at[index],
        recv_sem=sem_pair[1].at[index],
        device_id=(peer, t),
        device_id_type=MESH,
    )


class WeightGather:
    def __init__(self, dp, own, out, slow_sems, fast_sems):
        self.dp, self.half = dp, dp // 2
        self.own, self.out = own, out
        self.slow_sems, self.fast_sems = slow_sems, fast_sems
        self.d = lax.axis_index("dp")
        self.f = lax.rem(self.d, 2)
        self.partner = self.d + 1 - 2 * self.f

    def slow(self, k):
        peer = lax.rem(self.d + 2 * k, self.dp)
        return pair_copy(self.own, self.out.at[self.d], self.slow_sems, k, peer)

    def fast(self, k):
        if isinstance(k, int) and k == 0:
            return pair_copy(self.own, self.out.at[self.d], self.fast_sems, 0, self.partner)
        source = lax.rem(self.d + self.dp - 2 * k, self.dp)
        ref = self.out.at[source]
        return pair_copy(ref, ref, self.fast_sems, k, self.partner)

    def start(self):
        each_peer(self.half, lambda k: self.slow(k).start())
        self.fast(0).start()

    def forward(self):
        def step(k):
            self.slow(k).wait_recv()
            self.fast(k).start()

        each_peer(self.half, step)

    def finish(self):
        self.fast(0).wait()
        each_peer(self.half, lambda k: self.fast(k).wait())
        each_peer(self.half, lambda k: self.slow(k).wait_send())


class WeightScatter:
    def __init__(self, dp, part, near, total, far, slow_sems, fast_sems):
        self.dp, self.half = dp, dp // 2
        self.part, self.near, self.total, self.far = part, near, total, far
        self.slow_sems, self.fast_sems = slow_sems, fast_sems
        self.d = lax.axis_index("dp")
        self.f = lax.rem(self.d, 2)
        self.partner = self.d + 1 - 2 * self.f

    def fast(self, k):
        target = lax.rem(self.partner + 2 * k, self.dp)
        return pair_copy(
            self.part.at[target], self.near.at[k], self.fast_sems, k, self.partner
        )

    def slow(self, k):
        peer = lax.rem(self.d + 2 * k, self.dp)
        return pair_copy(self.total.at[k], self.far.at[k], self.slow_sems, k, peer)

    def start(self):
        each_peer(self.half, lambda k: self.fast(k).start())
        self.fast(0).start()

    def middle(self):
        def step(k):
            self.fast(k).wait_recv()
            target = lax.rem(self.d + 2 * k, self.dp)
            self.total[k] = (self.part[target].astype(F32) + self.near[k].astype(F32)).astype(
                BF16
            )
            self.slow(k).start()

        each_peer(self.half, step)

    def result(self):
        self.fast(0).wait_recv()
        acc = self.part[self.d].astype(F32) + self.near[0].astype(F32)
        for k in range(1, self.half):
            self.slow(k).wait_recv()
            acc = acc + self.far[k].astype(F32)
        return acc

    def finish(self):
        self.fast(0).wait_send()
        each_peer(self.half, lambda k: self.fast(k).wait_send())
        each_peer(self.half, lambda k: self.slow(k).wait_send())


def sem_pairs(dp):
    return [pltpu.SemaphoreType.DMA((dp // 2,)) for _ in range(4)]


def weight_scratch(dp, shard, width):
    return [pltpu.VMEM((dp // 2, shard, width), BF16) for _ in range(3)] + sem_pairs(dp)


def first_kernel(
    dp, x_ref, cot_ref, small_ref, pack_ref, inner_ref,
    gathered_ref, inner_all_ref, vec_ref, low_ref, cot_all_ref,
    small_buf, s_send, s_recv, own_sem, l_send, l_recv, c_send, c_recv,
    p0, p1, p2, p3, i0, i1, i2, i3,
):
    d, t, sib, opp, diag = places()
    owns = [
        pltpu.make_async_copy(pack_ref, gathered_ref.at[d], own_sem.at[0]),
        pltpu.make_async_copy(inner_ref, inner_all_ref.at[d], own_sem.at[1]),
    ]
    for own in owns:
        own.start()
    small_buf[d] = small_ref[...]
    greet(dp, (sib, opp))

    def small_copy(k):
        return dp_copy(dp, k, small_buf.at[d], small_buf.at[d], s_send, s_recv)

    pack = WeightGather(dp, pack_ref, gathered_ref, (p0, p1), (p2, p3))
    inner = WeightGather(dp, inner_ref, inner_all_ref, (i0, i1), (i2, i3))
    each_peer(dp, lambda k: small_copy(k).start())
    pack.start()
    inner.start()
    low = Gather(low_ref, l_send, l_recv)
    cot = Gather(cot_all_ref, c_send, c_recv)
    each_peer(dp, lambda k: small_copy(k).wait_recv())
    vec_ref[...] = jnp.sum(small_buf[...], axis=0)
    gain, shift = vec_ref[0:1, :], vec_ref[1:2, :]
    for c in range(low.chunks):
        normed, _ = normed_rows(x_ref[rows_of(c), :])
        low_ref[t, rows_of(c), :] = (normed * gain + shift).astype(BF16)
        low.start(c)
    for c in range(cot.chunks):
        cot_all_ref[t, rows_of(c), :] = cot_ref[rows_of(c), :].astype(BF16)
        cot.start(c)
    pack.forward()
    for c in range(low.chunks):
        low.forward(c)
    inner.forward()
    for c in range(cot.chunks):
        cot.forward(c)
    low.finish()
    cot.finish()
    each_peer(dp, lambda k: small_copy(k).wait_send())
    pack.finish()
    inner.finish()
    for own in owns:
        own.wait()


def second_kernel(
    dp, part_ref, x_ref, vec_ref, outer_ref,
    mixed_ref, low_ref, outer_all_ref,
    near, total, far, r_send, r_recv, l_send, l_recv,
    own_sem, o0, o1, o2, o3,
):
    d, t, sib, opp, diag = places()
    own = pltpu.make_async_copy(outer_ref, outer_all_ref.at[d], own_sem)
    own.start()
    greet(dp, (sib, opp))
    scat = Scatter(part_ref, near, total, far, r_send, r_recv)
    low = Gather(low_ref, l_send, l_recv)
    outer = WeightGather(dp, outer_ref, outer_all_ref, (o0, o1), (o2, o3))
    scat.start()
    outer.start()
    for c in range(scat.chunks):
        scat.middle(c)
    bias, gain, shift = vec_ref[2:3, :], vec_ref[3:4, :], vec_ref[4:5, :]
    for c in range(scat.chunks):
        mixed = x_ref[rows_of(c), :] + scat.result(c) + bias
        mixed_ref[rows_of(c), :] = mixed
        normed, _ = normed_rows(mixed)
        low_ref[t, rows_of(c), :] = (normed * gain + shift).astype(BF16)
        low.start(c)
    outer.forward()
    for c in range(low.chunks):
        low.forward(c)
    low.finish()
    scat.finish()
    outer.finish()
    own.wait()


def third_kernel(
    dp, npart_ref, fpart_ref, mixed_ref, cot_ref, vec_ref, wo_ref, wi_ref,
    grad_ref, all_ref, out_ref, sums_ref, wo_out_ref, wi_out_ref,
    n_near, n_total, n_far, n_send, n_recv,
    f_near, f_total, f_far, f_send, f_recv,
    g_send, g_recv,
    o_near, o_total, o_far, o0, o1, o2, o3,
    i_near, i_total, i_far, i0, i1, i2, i3,
):
    d, t, sib, opp, diag = places()
    greet(dp, (sib, opp))
    outer = WeightScatter(dp, wo_ref, o_near, o_total, o_far, (o0, o1), (o2, o3))
    inner = WeightScatter(dp, wi_ref, i_near, i_total, i_far, (i0, i1), (i2, i3))
    first = Scatter(npart_ref, n_near, n_total, n_far, n_send, n_recv)
    feed = Scatter(fpart_ref, f_near, f_total, f_far, f_send, f_recv)
    gather = Gather(all_ref, g_send, g_recv)
    first.start()
    outer.start()
    inner.start()
    for c in range(first.chunks):
        first.middle(c)
    feed.start()
    gain = vec_ref[3:4, :]
    sums = [jnp.zeros_like(gain) for _ in range(4)]
    for c in range(first.chunks):
        gradient = first.result(c)
        cot = cot_ref[rows_of(c), :]
        normed, rstd = normed_rows(mixed_ref[rows_of(c), :])
        mixed_grad = cot + norm_back(gradient, normed, rstd, gain)
        grad_ref[rows_of(c), :] = mixed_grad
        all_ref[t, rows_of(c), :] = mixed_grad.astype(BF16)
        gather.start(c)
        terms = (mixed_grad, gradient * normed, gradient, cot)
        sums = [s + jnp.sum(v, axis=0, keepdims=True) for s, v in zip(sums, terms)]
    zero = jnp.zeros_like(gain)
    sums_ref[...] = jnp.concatenate([zero, zero] + sums + [zero, zero], axis=0)
    for c in range(feed.chunks):
        feed.middle(c)
    outer.middle()
    for c in range(gather.chunks):
        gather.forward(c)
    inner.middle()
    bias = vec_ref[5:6, :]
    for c in range(feed.chunks):
        out_ref[rows_of(c), :] = mixed_ref[rows_of(c), :] + feed.result(c) + bias
    gather.finish()
    wo_out_ref[...] = outer.result()
    wi_out_ref[...] = inner.result()
    first.finish()
    feed.finish()
    outer.finish()
    inner.finish()


def fourth_kernel(
    dp, part_ref, x_ref, mixed_grad_ref, vec_ref, sums_ref, wgrad_ref,
    input_grad_ref, wout_ref, vout_ref,
    near, total, far, r_send, r_recv,
    w_near, w_total, w_far, w0, w1, w2, w3, group, t_send, t_recv, whole, v_send, v_recv,
):
    d, t, sib, opp, diag = places()
    greet(dp, (sib, opp, diag))
    scat = Scatter(part_ref, near, total, far, r_send, r_recv)
    scat.start()

    weights = WeightScatter(dp, wgrad_ref, w_near, w_total, w_far, (w0, w1), (w2, w3))
    weights.start()
    for c in range(scat.chunks):
        scat.middle(c)
    weights.middle()
    gain = vec_ref[0:1, :]
    sums = [jnp.zeros_like(gain) for _ in range(2)]
    for c in range(scat.chunks):
        gradient = scat.result(c)
        normed, rstd = normed_rows(x_ref[rows_of(c), :])
        input_grad_ref[rows_of(c), :] = mixed_grad_ref[rows_of(c), :] + norm_back(
            gradient, normed, rstd, gain
        )
        terms = (gradient * normed, gradient)
        sums = [s + jnp.sum(v, axis=0, keepdims=True) for s, v in zip(sums, terms)]
    mine = sums_ref[...] + jnp.concatenate(
        sums + [jnp.zeros((VROWS - 2, gain.shape[1]), F32)], axis=0
    )
    group[t] = mine
    tensor_copies = [
        pltpu.make_async_remote_copy(
            src_ref=group.at[t],
            dst_ref=group.at[t],
            send_sem=t_send.at[i],
            recv_sem=t_recv.at[i],
            device_id=(d, peer),
            device_id_type=MESH,
        )
        for i, peer in enumerate((sib, opp, diag))
    ]
    for copy in tensor_copies:
        copy.start()
    for copy in tensor_copies:
        copy.wait()
    over_group = jnp.sum(group[...], axis=0)
    row = lax.broadcasted_iota(jnp.int32, mine.shape, 0)
    whole[d] = jnp.where(row < 6, over_group, mine)

    def vector_copy(k):
        return dp_copy(dp, k, whole.at[d], whole.at[d], v_send, v_recv)

    each_peer(dp, lambda k: vector_copy(k).start())
    wout_ref[...] = weights.result()
    each_peer(dp, lambda k: vector_copy(k).wait())
    vout_ref[...] = jnp.sum(whole[...], axis=0)
    scat.finish()
    weights.finish()


VM = pl.BlockSpec(memory_space=pltpu.VMEM)
ANY = pl.BlockSpec(memory_space=pl.ANY)


def comm_call(kernel, ident, in_specs, outs, out_specs, scratch, flops=20_000_000_000):
    return pl.pallas_call(
        kernel,
        out_shape=tuple(jax.ShapeDtypeStruct(s, dt) for s, dt in outs),
        in_specs=in_specs,
        out_specs=tuple(out_specs),
        scratch_shapes=scratch,
        cost_estimate=pl.CostEstimate(flops=flops, bytes_accessed=4_000_000, transcendentals=0),
        compiler_params=pltpu.CompilerParams(
            collective_id=ident, has_side_effects=True, vmem_limit_bytes=36 * 1024 * 1024
        ),
    )


def token_kernel(a_ref, b_ref, o_ref):
    o_ref[...] = lax.dot_general(
        a_ref[...], b_ref[...], (((0,), (0,)), ((), ())), preferred_element_type=F32
    ).astype(o_ref.dtype)


def token_product(left, right):
    tokens, m = left.shape
    n = right.shape[1]
    tile = 256
    return pl.pallas_call(
        token_kernel,
        grid=(m // tile,),
        out_shape=jax.ShapeDtypeStruct((m, n), BF16),
        in_specs=[
            pl.BlockSpec((tokens, tile), lambda i: (0, i)),
            pl.BlockSpec((tokens, n), lambda i: (0, 0)),
        ],
        out_specs=pl.BlockSpec((tile, n), lambda i: (i, 0)),
        cost_estimate=pl.CostEstimate(
            flops=2 * tokens * m * n, bytes_accessed=2 * (tokens * (m + n) + m * n), transcendentals=0
        ),
        compiler_params=pltpu.CompilerParams(vmem_limit_bytes=24 * 1024 * 1024),
    )(left, right)


def attend(operands):
    queries, key_rows, values = operands
    score_scale = 1.0 / math.sqrt(HD)
    scores = (
        jnp.einsum(
            "qhd,khd->hqk",
            split_heads(queries),
            split_heads(key_rows),
            preferred_element_type=jnp.float32,
        )
        * score_scale
    )
    row_max = jnp.max(scores, axis=-1, keepdims=True)
    log_total = row_max + jnp.log(jnp.sum(jnp.exp(scores - row_max), axis=-1, keepdims=True))
    prob_low = jnp.exp(scores - log_total).astype(jnp.bfloat16)
    context = jnp.einsum(
        "hqk,khd->qhd", prob_low, split_heads(values), preferred_element_type=jnp.float32
    )
    return (context.reshape(queries.shape).astype(jnp.bfloat16), log_total)


def attend_back_kernel(heads, qkv_ref, grad_ref, log_ref, out_ref, sums_ref, queries_t, keys, vals):
    scale = 1.0 / math.sqrt(HD)
    width = heads * HD
    frames = qkv_ref.shape[0]
    tile = 256
    for h in range(heads):
        lanes = slice(h * HD, (h + 1) * HD)
        key = qkv_ref[:, width + h * HD : width + (h + 1) * HD]
        value = qkv_ref[:, 2 * width + h * HD : 2 * width + (h + 1) * HD]
        key_t = key.astype(F32).T.astype(BF16)
        keys[...] = jnp.zeros_like(keys)
        vals[...] = jnp.zeros_like(vals)

        def step(i, carry, lanes=lanes, key=key, value=value, key_t=key_t, h=h):
            start = pl.multiple_of(i * tile, tile)
            at = pl.ds(start, tile)
            query = qkv_ref[at, lanes]
            grad = grad_ref[at, lanes]
            scores = matmul_nt(key, query) * scale
            prob = jnp.exp(scores - log_ref[h : h + 1, at])
            vals[...] += matmul(prob.astype(BF16), grad)
            prob_grad = matmul_nt(value, grad)
            row_dot = jnp.sum(prob * prob_grad, axis=0, keepdims=True)
            score_grad = (prob * (prob_grad - row_dot) * scale).astype(BF16)
            keys[...] += matmul(score_grad, query)
            queries_t[lanes, at] = matmul(key_t, score_grad)
            return carry

        lax.fori_loop(0, frames // tile, step, 0)
        value_grad = vals[...]
        out_ref[:, width + h * HD : width + (h + 1) * HD] = keys[...].astype(BF16)
        out_ref[:, 2 * width + h * HD : 2 * width + (h + 1) * HD] = value_grad.astype(BF16)
        query_grad = queries_t[lanes, :].T
        out_ref[:, lanes] = query_grad.astype(BF16)
        sums_ref[0:1, lanes] = jnp.sum(query_grad, axis=0, keepdims=True)
        sums_ref[1:2, lanes] = jnp.sum(value_grad, axis=0, keepdims=True)


def attend_back(qkv, context_grad, log_total):
    clips, frames, wide = qkv.shape
    width = context_grad.shape[2]
    heads = width // HD

    def spec(*shape):
        return pl.BlockSpec((None,) + shape, lambda c: (c, 0, 0))

    return pl.pallas_call(
        functools.partial(attend_back_kernel, heads),
        grid=(clips,),
        out_shape=(
            jax.ShapeDtypeStruct((clips, frames, wide), BF16),
            jax.ShapeDtypeStruct((clips, 2, width), F32),
        ),
        in_specs=[spec(frames, wide), spec(frames, width), spec(heads, frames)],
        out_specs=(spec(frames, wide), spec(2, width)),
        scratch_shapes=[
            pltpu.VMEM((width, frames), F32),
            pltpu.VMEM((frames, HD), F32),
            pltpu.VMEM((frames, HD), F32),
        ],
        cost_estimate=pl.CostEstimate(
            flops=10 * clips * heads * frames * frames * HD,
            bytes_accessed=6_000_000,
            transcendentals=clips * heads * frames * frames,
        ),
        compiler_params=pltpu.CompilerParams(vmem_limit_bytes=36 * 1024 * 1024),
    )(qkv, context_grad, log_total)


def on_device(
    dp,
    layer_input,
    out_cotangent,
    mix_gain,
    mix_shift,
    query_weight,
    query_bias,
    key_weight,
    value_weight,
    value_bias,
    output_weight,
    output_bias,
    feed_gain,
    feed_shift,
    inner_weight,
    inner_bias,
    outer_weight,
    outer_bias,
):
    d = lax.axis_index("dp")
    t = lax.axis_index("tensor")
    clips, share, feats = layer_input.shape
    rows = clips * share
    frames = share * 4
    width = query_weight.shape[1]
    shard = query_weight.shape[0]
    hidden_units = inner_weight.shape[1]

    def placed_bias(bias):
        full = jnp.zeros((HD, bias.shape[1]), F32)
        full = lax.dynamic_update_slice(full, bias.astype(F32), (d * bias.shape[0], 0))
        return full.T.reshape(-1)

    vectors = jnp.stack([mix_gain, mix_shift, output_bias, feed_gain, feed_shift, outer_bias])
    upper = lax.dynamic_update_slice(
        jnp.zeros((6, feats), F32), vectors.astype(F32), (0, d * vectors.shape[1])
    )
    none = jnp.zeros((width,), F32)
    head_row = jnp.concatenate([placed_bias(query_bias), none, placed_bias(value_bias), none])
    small = jnp.concatenate([upper, head_row[None], placed_bias(inner_bias)[None]], axis=0)
    pack = jnp.concatenate([query_weight, key_weight, value_weight, output_weight], axis=1)

    x = layer_input.reshape(rows, feats)
    cot = out_cotangent.reshape(rows, feats)
    block = (4, rows, feats)

    def to_tokens(gathered):
        return (
            gathered.reshape(4, clips, share, feats)
            .transpose(1, 0, 2, 3)
            .reshape(clips * frames, feats)
        )

    def to_blocks(tokens):
        return (
            tokens.astype(BF16)
            .reshape(clips, 4, share, feats)
            .transpose(1, 0, 2, 3)
            .reshape(block)
        )

    gathered_pack, inner_all, vec, low_one, cot_all = comm_call(
        functools.partial(first_kernel, dp),
        1,
        [VM, VM, VM, ANY, ANY],
        [((dp,) + pack.shape, BF16), ((dp,) + inner_weight.shape, BF16), ((VROWS, feats), F32), (block, BF16), (block, BF16)],
        [ANY, ANY, VM, VM, VM],
        [
            pltpu.VMEM((dp, VROWS, feats), F32),
            pltpu.SemaphoreType.DMA((dp,)),
            pltpu.SemaphoreType.DMA((dp,)),
            pltpu.SemaphoreType.DMA((2,)),
        ]
        + gather_scratch(rows)
        + gather_scratch(rows)
        + sem_pairs(dp)
        + sem_pairs(dp),
    )(x, cot, small, pack, inner_weight)
    inner_full = inner_all.reshape(feats, hidden_units)
    flat_one = to_tokens(low_one)
    cot_tokens = to_tokens(cot_all)
    attn_weights = gathered_pack.reshape(feats, 4 * width)
    qkv_full = attn_weights[:, : 3 * width]
    output_full = attn_weights[:, 3 * width :]
    qkv = (matmul(flat_one, qkv_full) + vec[6, : 3 * width]).astype(BF16)
    clip_qkv = qkv.reshape(clips, frames, 3 * width)
    clip_queries = clip_qkv[:, :, :width]
    clip_keys = clip_qkv[:, :, width : 2 * width]
    clip_values = clip_qkv[:, :, 2 * width :]
    context, log_total = lax.map(attend, (clip_queries, clip_keys, clip_values))
    flat_context = context.reshape(clips * frames, width)
    attn_part = to_blocks(matmul_nt(flat_context, output_full))

    mixed, low_two, outer_all = comm_call(
        functools.partial(second_kernel, dp),
        2,
        [VM, VM, VM, ANY],
        [((rows, feats), F32), (block, BF16), ((dp,) + outer_weight.shape, BF16)],
        [VM, VM, ANY],
        scatter_scratch(rows, feats)
        + gather_scratch(rows)
        + [pltpu.SemaphoreType.DMA]
        + sem_pairs(dp),
    )(attn_part, x, vec, outer_weight)
    outer_full = outer_all.reshape(feats, hidden_units)
    flat_two = to_tokens(low_two)
    preact = matmul(flat_two, inner_full) + vec[7, :hidden_units]
    hidden = gelu_value(preact).astype(BF16)
    preact_grad = matmul(cot_tokens, outer_full) * gelu_slope(preact)
    preact_low = preact_grad.astype(BF16)
    inner_bias_sum = jnp.sum(preact_grad, axis=0)
    norm_two_part = to_blocks(matmul_nt(preact_low, inner_full))
    feed_part = to_blocks(matmul_nt(hidden, outer_full))

    outer_part = token_product(cot_tokens, hidden)
    inner_part = token_product(flat_two, preact_low)
    by_shard = (dp, shard, hidden_units)

    (
        mixed_grad, mixed_all, layer_output, sums, outer_weight_grad, inner_weight_grad,
    ) = comm_call(
        functools.partial(third_kernel, dp),
        3,
        [VM] * 7,
        [
            ((rows, feats), F32),
            (block, BF16),
            ((rows, feats), F32),
            ((VROWS, feats), F32),
            ((shard, hidden_units), F32),
            ((shard, hidden_units), F32),
        ],
        [VM] * 6,
        scatter_scratch(rows, feats)
        + scatter_scratch(rows, feats)
        + gather_scratch(rows)
        + weight_scratch(dp, shard, hidden_units)
        + weight_scratch(dp, shard, hidden_units),
    )(
        norm_two_part, feed_part, mixed, cot, vec,
        outer_part.reshape(by_shard), inner_part.reshape(by_shard),
    )
    mixed_tokens = to_tokens(mixed_all)
    output_part = token_product(mixed_tokens, flat_context)
    context_grad = matmul(mixed_tokens, output_full).astype(BF16).reshape(clips, frames, width)
    low_grads, head_sums = attend_back(
        clip_qkv, context_grad, log_total.reshape(clips, width // HD, frames)
    )
    low_grads = low_grads.reshape(clips * frames, 3 * width)
    head_sums = jnp.sum(head_sums, axis=0)
    norm_one_part = to_blocks(matmul_nt(low_grads, qkv_full))
    attn_wpart = jnp.concatenate([token_product(flat_one, low_grads), output_part], axis=1)
    bias_row = jnp.concatenate(
        [head_sums[0], none, head_sums[1], none]
    )
    sums = sums + jnp.concatenate(
        [jnp.zeros((VROWS - 2, feats), F32), bias_row[None], inner_bias_sum[None]], axis=0
    )

    input_grad, attn_grads, vector_sums = comm_call(
        functools.partial(fourth_kernel, dp),
        4,
        [VM] * 6,
        [((rows, feats), F32), ((shard, 4 * width), F32), ((VROWS, feats), F32)],
        [VM] * 3,
        scatter_scratch(rows, feats)
        + weight_scratch(dp, shard, 4 * width)
        + [
            pltpu.VMEM((4, VROWS, feats), F32),
            pltpu.SemaphoreType.DMA((3,)),
            pltpu.SemaphoreType.DMA((3,)),
            pltpu.VMEM((dp, VROWS, feats), F32),
            pltpu.SemaphoreType.DMA((dp,)),
            pltpu.SemaphoreType.DMA((dp,)),
        ],
    )(norm_one_part, x, mixed_grad, vec, sums, attn_wpart.reshape(dp, shard, 4 * width))

    piece = feats // (4 * dp)
    mine = lax.dynamic_slice(vector_sums, (0, (d * 4 + t) * piece), (VROWS, piece))

    def bias_share(vector, like):
        table = vector.reshape(-1, HD).T
        return lax.dynamic_slice(table, (d * like.shape[0], 0), like.shape)

    return (
        layer_output.reshape(layer_input.shape),
        input_grad.reshape(layer_input.shape),
        mine[0],
        mine[1],
        attn_grads[:, :width],
        bias_share(vector_sums[6, :width], query_bias),
        attn_grads[:, width : 2 * width],
        attn_grads[:, 2 * width : 3 * width],
        bias_share(vector_sums[6, 2 * width : 3 * width], value_bias),
        attn_grads[:, 3 * width :],
        mine[2],
        mine[3],
        mine[4],
        inner_weight_grad,
        bias_share(vector_sums[7, :hidden_units], inner_bias),
        outer_weight_grad,
        mine[5],
    )


def solution(mesh):
    placed = (
        P("dp", "tensor", None),
        P("dp", "tensor", None),
        P("dp"),
        P("dp"),
        P("dp", "tensor"),
        P("dp", "tensor"),
        P("dp", "tensor"),
        P("dp", "tensor"),
        P("dp", "tensor"),
        P("dp", "tensor"),
        P("dp"),
        P("dp"),
        P("dp"),
        P("dp", "tensor"),
        P("dp", "tensor"),
        P("dp", "tensor"),
        P("dp"),
    )
    return jax.shard_map(
        functools.partial(on_device, mesh.shape["dp"]),
        mesh=mesh,
        in_specs=placed,
        out_specs=(
            P("dp", "tensor", None),
            P("dp", "tensor", None),
            P(("dp", "tensor")),
            P(("dp", "tensor")),
            P("dp", "tensor"),
            P("dp", "tensor"),
            P("dp", "tensor"),
            P("dp", "tensor"),
            P("dp", "tensor"),
            P("dp", "tensor"),
            P(("dp", "tensor")),
            P(("dp", "tensor")),
            P(("dp", "tensor")),
            P("dp", "tensor"),
            P("dp", "tensor"),
            P("dp", "tensor"),
            P(("dp", "tensor")),
        ),
        check_vma=False,
    )
```

```python
import functools
import math

import jax
import jax.numpy as jnp
from jax import lax
from jax.experimental import pallas as pl
from jax.experimental.pallas import tpu as pltpu
from jax.sharding import PartitionSpec as P

HD = 64
EPS = 1e-05
ROOT_HALF = 0.7071067811865476
DENSITY_NORM = 0.3989422804014327
MESH = pl.DeviceIdType.MESH
CHUNK = 64
VROWS = 8
F32 = jnp.float32
BF16 = jnp.bfloat16


def gelu_value(preact):
    return 0.5 * preact * (1.0 + lax.erf(preact * ROOT_HALF))


def gelu_slope(preact):
    return 0.5 * (1.0 + lax.erf(preact * ROOT_HALF)) + preact * DENSITY_NORM * jnp.exp(
        -0.5 * preact * preact
    )


def matmul(left, right):
    return jnp.dot(left, right, preferred_element_type=F32)


def matmul_nt(left, right):
    return lax.dot_general(left, right, (((1,), (1,)), ((), ())), preferred_element_type=F32)


def split_heads(block):
    return block.reshape(block.shape[0], block.shape[1] // HD, HD)


def places():
    d = lax.axis_index("dp")
    t = lax.axis_index("tensor")
    sib = t + 1 - 2 * lax.rem(t, 2)
    opp = lax.rem(t + 2, 4)
    diag = lax.rem(sib + 2, 4)
    return d, t, sib, opp, diag


def greet(dp, tensor_peers):
    d, t = lax.axis_index("dp"), lax.axis_index("tensor")
    barrier = pltpu.get_barrier_semaphore()
    for peer in tensor_peers:
        pl.semaphore_signal(barrier, inc=1, device_id=(d, peer), device_id_type=MESH)

    def signal(k):
        pl.semaphore_signal(
            barrier, inc=1, device_id=(lax.rem(d + k, dp), t), device_id_type=MESH
        )

    each_peer(dp, signal)
    pl.semaphore_wait(barrier, len(tensor_peers) + dp - 1)


def normed_rows(block):
    row_mean = jnp.mean(block, axis=-1, keepdims=True)
    centred = block - row_mean
    rstd = lax.rsqrt(jnp.mean(centred * centred, axis=-1, keepdims=True) + EPS)
    return centred * rstd, rstd


def norm_back(gradient, normed, rstd, gain):
    scaled = gradient * gain
    first = jnp.mean(scaled, axis=-1, keepdims=True)
    second = jnp.mean(scaled * normed, axis=-1, keepdims=True)
    return (scaled - first - normed * second) * rstd


def rows_of(c):
    return pl.ds(c * CHUNK, CHUNK)


class Gather:
    def __init__(self, buf, send, recv):
        self.buf, self.send, self.recv = buf, send, recv
        self.chunks = buf.shape[1] // CHUNK

    def copy(self, slot, kind, c, peer):
        d = lax.axis_index("dp")
        ref = self.buf.at[slot, rows_of(c)]
        return pltpu.make_async_remote_copy(
            src_ref=ref,
            dst_ref=ref,
            send_sem=self.send.at[kind, c],
            recv_sem=self.recv.at[kind, c],
            device_id=(d, peer),
            device_id_type=MESH,
        )

    def start(self, c):
        _, t, sib, opp, _ = places()
        self.copy(t, 1, c, opp).start()
        self.copy(t, 0, c, sib).start()

    def forward(self, c):
        _, t, sib, opp, _ = places()
        self.copy(opp, 1, c, opp).wait_recv()
        self.copy(opp, 2, c, sib).start()

    def finish(self):
        _, t, sib, opp, diag = places()
        for c in range(self.chunks):
            self.copy(sib, 0, c, sib).wait_recv()
            self.copy(diag, 2, c, sib).wait_recv()
        for c in range(self.chunks):
            self.copy(t, 0, c, sib).wait_send()
            self.copy(t, 1, c, opp).wait_send()
            self.copy(opp, 2, c, sib).wait_send()


class Scatter:
    def __init__(self, part, near, total, far, send, recv):
        self.part, self.near, self.total, self.far = part, near, total, far
        self.send, self.recv = send, recv
        self.chunks = part.shape[1] // CHUNK

    def copy(self, src, dst, kind, c, peer):
        d = lax.axis_index("dp")
        return pltpu.make_async_remote_copy(
            src_ref=src,
            dst_ref=dst,
            send_sem=self.send.at[kind, c],
            recv_sem=self.recv.at[kind, c],
            device_id=(d, peer),
            device_id_type=MESH,
        )

    def to_sibling(self, kind, c):
        _, _, sib, _, diag = places()
        block = sib if kind == 0 else diag
        return self.copy(
            self.part.at[block, rows_of(c)], self.near.at[kind, rows_of(c)], kind, c, sib
        )

    def across(self, c):
        _, _, _, opp, _ = places()
        return self.copy(self.total.at[rows_of(c)], self.far.at[rows_of(c)], 2, c, opp)

    def start(self):
        for c in range(self.chunks):
            self.to_sibling(1, c).start()
        for c in range(self.chunks):
            self.to_sibling(0, c).start()

    def middle(self, c):
        _, _, _, opp, _ = places()
        self.to_sibling(1, c).wait_recv()
        rows = rows_of(c)
        self.total[rows, :] = (
            self.part[opp, rows, :].astype(F32) + self.near[1, rows, :].astype(F32)
        ).astype(BF16)
        self.across(c).start()

    def result(self, c):
        _, t, _, _, _ = places()
        self.to_sibling(0, c).wait_recv()
        self.across(c).wait_recv()
        rows = rows_of(c)
        return (
            self.part[t, rows, :].astype(F32)
            + self.near[0, rows, :].astype(F32)
            + self.far[rows, :].astype(F32)
        )

    def finish(self):
        for c in range(self.chunks):
            self.to_sibling(0, c).wait_send()
            self.to_sibling(1, c).wait_send()
            self.across(c).wait_send()


def scatter_scratch(rows, width):
    return [
        pltpu.VMEM((2, rows, width), BF16),
        pltpu.VMEM((rows, width), BF16),
        pltpu.VMEM((rows, width), BF16),
        pltpu.SemaphoreType.DMA((3, rows // CHUNK)),
        pltpu.SemaphoreType.DMA((3, rows // CHUNK)),
    ]


def gather_scratch(rows):
    return [
        pltpu.SemaphoreType.DMA((3, rows // CHUNK)),
        pltpu.SemaphoreType.DMA((3, rows // CHUNK)),
    ]


def dp_copy(dp, k, src, dst, send, recv):
    d, t = lax.axis_index("dp"), lax.axis_index("tensor")
    return pltpu.make_async_remote_copy(
        src_ref=src,
        dst_ref=dst,
        send_sem=send.at[k],
        recv_sem=recv.at[k],
        device_id=(lax.rem(d + k, dp), t),
        device_id_type=MESH,
    )


def each_peer(dp, body):
    def step(k, carry):
        body(k)
        return carry

    lax.fori_loop(1, dp, step, 0)


def pair_copy(src, dst, sem_pair, index, peer):
    t = lax.axis_index("tensor")
    return pltpu.make_async_remote_copy(
        src_ref=src,
        dst_ref=dst,
        send_sem=sem_pair[0].at[index],
        recv_sem=sem_pair[1].at[index],
        device_id=(peer, t),
        device_id_type=MESH,
    )


class WeightGather:
    def __init__(self, dp, own, out, slow_sems, fast_sems):
        self.dp, self.half = dp, dp // 2
        self.own, self.out = own, out
        self.slow_sems, self.fast_sems = slow_sems, fast_sems
        self.d = lax.axis_index("dp")
        self.f = lax.rem(self.d, 2)
        self.partner = self.d + 1 - 2 * self.f

    def slow(self, k):
        peer = lax.rem(self.d + 2 * k, self.dp)
        return pair_copy(self.own, self.out.at[self.d], self.slow_sems, k, peer)

    def fast(self, k):
        if isinstance(k, int) and k == 0:
            return pair_copy(self.own, self.out.at[self.d], self.fast_sems, 0, self.partner)
        source = lax.rem(self.d + self.dp - 2 * k, self.dp)
        ref = self.out.at[source]
        return pair_copy(ref, ref, self.fast_sems, k, self.partner)

    def start(self):
        each_peer(self.half, lambda k: self.slow(k).start())
        self.fast(0).start()

    def forward(self):
        def step(k):
            self.slow(k).wait_recv()
            self.fast(k).start()

        each_peer(self.half, step)

    def finish(self):
        self.fast(0).wait()
        each_peer(self.half, lambda k: self.fast(k).wait())
        each_peer(self.half, lambda k: self.slow(k).wait_send())


class WeightScatter:
    def __init__(self, dp, part, near, total, far, slow_sems, fast_sems):
        self.dp, self.half = dp, dp // 2
        self.part, self.near, self.total, self.far = part, near, total, far
        self.slow_sems, self.fast_sems = slow_sems, fast_sems
        self.d = lax.axis_index("dp")
        self.f = lax.rem(self.d, 2)
        self.partner = self.d + 1 - 2 * self.f

    def fast(self, k):
        target = lax.rem(self.partner + 2 * k, self.dp)
        return pair_copy(
            self.part.at[target], self.near.at[k], self.fast_sems, k, self.partner
        )

    def slow(self, k):
        peer = lax.rem(self.d + 2 * k, self.dp)
        return pair_copy(self.total.at[k], self.far.at[k], self.slow_sems, k, peer)

    def start(self):
        each_peer(self.half, lambda k: self.fast(k).start())
        self.fast(0).start()

    def middle(self):
        def step(k):
            self.fast(k).wait_recv()
            target = lax.rem(self.d + 2 * k, self.dp)
            self.total[k] = (self.part[target].astype(F32) + self.near[k].astype(F32)).astype(
                BF16
            )
            self.slow(k).start()

        each_peer(self.half, step)

    def result(self):
        self.fast(0).wait_recv()
        acc = self.part[self.d].astype(F32) + self.near[0].astype(F32)
        for k in range(1, self.half):
            self.slow(k).wait_recv()
            acc = acc + self.far[k].astype(F32)
        return acc

    def finish(self):
        self.fast(0).wait_send()
        each_peer(self.half, lambda k: self.fast(k).wait_send())
        each_peer(self.half, lambda k: self.slow(k).wait_send())


def sem_pairs(dp):
    return [pltpu.SemaphoreType.DMA((dp // 2,)) for _ in range(4)]


def weight_scratch(dp, shard, width):
    return [pltpu.VMEM((dp // 2, shard, width), BF16) for _ in range(3)] + sem_pairs(dp)


def first_kernel(
    dp, x_ref, cot_ref, small_ref, pack_ref, inner_ref,
    gathered_ref, inner_all_ref, vec_ref, low_ref, cot_all_ref,
    small_buf, s_send, s_recv, own_sem, l_send, l_recv, c_send, c_recv,
    p0, p1, p2, p3, i0, i1, i2, i3,
):
    d, t, sib, opp, diag = places()
    owns = [
        pltpu.make_async_copy(pack_ref, gathered_ref.at[d], own_sem.at[0]),
        pltpu.make_async_copy(inner_ref, inner_all_ref.at[d], own_sem.at[1]),
    ]
    for own in owns:
        own.start()
    small_buf[d] = small_ref[...]
    greet(dp, (sib, opp))

    def small_copy(k):
        return dp_copy(dp, k, small_buf.at[d], small_buf.at[d], s_send, s_recv)

    pack = WeightGather(dp, pack_ref, gathered_ref, (p0, p1), (p2, p3))
    inner = WeightGather(dp, inner_ref, inner_all_ref, (i0, i1), (i2, i3))
    each_peer(dp, lambda k: small_copy(k).start())
    pack.start()
    inner.start()
    low = Gather(low_ref, l_send, l_recv)
    cot = Gather(cot_all_ref, c_send, c_recv)
    for c in range(cot.chunks):
        cot_all_ref[t, rows_of(c), :] = cot_ref[rows_of(c), :].astype(BF16)
        cot.start(c)
    each_peer(dp, lambda k: small_copy(k).wait_recv())
    vec_ref[...] = jnp.sum(small_buf[...], axis=0)
    gain, shift = vec_ref[0:1, :], vec_ref[1:2, :]
    for c in range(low.chunks):
        normed, _ = normed_rows(x_ref[rows_of(c), :])
        low_ref[t, rows_of(c), :] = (normed * gain + shift).astype(BF16)
        low.start(c)
    pack.forward()
    for c in range(low.chunks):
        low.forward(c)
    inner.forward()
    for c in range(cot.chunks):
        cot.forward(c)
    low.finish()
    cot.finish()
    each_peer(dp, lambda k: small_copy(k).wait_send())
    pack.finish()
    inner.finish()
    for own in owns:
        own.wait()


def second_kernel(
    dp, part_ref, x_ref, vec_ref, outer_ref,
    mixed_ref, low_ref, outer_all_ref,
    near, total, far, r_send, r_recv, l_send, l_recv,
    own_sem, o0, o1, o2, o3,
):
    d, t, sib, opp, diag = places()
    own = pltpu.make_async_copy(outer_ref, outer_all_ref.at[d], own_sem)
    own.start()
    greet(dp, (sib, opp))
    scat = Scatter(part_ref, near, total, far, r_send, r_recv)
    low = Gather(low_ref, l_send, l_recv)
    outer = WeightGather(dp, outer_ref, outer_all_ref, (o0, o1), (o2, o3))
    scat.start()
    outer.start()
    for c in range(scat.chunks):
        scat.middle(c)
    bias, gain, shift = vec_ref[2:3, :], vec_ref[3:4, :], vec_ref[4:5, :]
    for c in range(scat.chunks):
        mixed = x_ref[rows_of(c), :] + scat.result(c) + bias
        mixed_ref[rows_of(c), :] = mixed
        normed, _ = normed_rows(mixed)
        low_ref[t, rows_of(c), :] = (normed * gain + shift).astype(BF16)
        low.start(c)
    outer.forward()
    for c in range(low.chunks):
        low.forward(c)
    low.finish()
    scat.finish()
    outer.finish()
    own.wait()


def third_kernel(
    dp, npart_ref, fpart_ref, mixed_ref, cot_ref, vec_ref, wo_ref, wi_ref,
    grad_ref, all_ref, out_ref, sums_ref, wo_out_ref, wi_out_ref,
    n_near, n_total, n_far, n_send, n_recv,
    f_near, f_total, f_far, f_send, f_recv,
    g_send, g_recv,
    o_near, o_total, o_far, o0, o1, o2, o3,
    i_near, i_total, i_far, i0, i1, i2, i3,
):
    d, t, sib, opp, diag = places()
    greet(dp, (sib, opp))
    outer = WeightScatter(dp, wo_ref, o_near, o_total, o_far, (o0, o1), (o2, o3))
    inner = WeightScatter(dp, wi_ref, i_near, i_total, i_far, (i0, i1), (i2, i3))
    first = Scatter(npart_ref, n_near, n_total, n_far, n_send, n_recv)
    feed = Scatter(fpart_ref, f_near, f_total, f_far, f_send, f_recv)
    gather = Gather(all_ref, g_send, g_recv)
    first.start()
    outer.start()
    inner.start()
    for c in range(first.chunks):
        first.middle(c)
    feed.start()
    gain = vec_ref[3:4, :]
    sums = [jnp.zeros_like(gain) for _ in range(4)]
    for c in range(first.chunks):
        gradient = first.result(c)
        cot = cot_ref[rows_of(c), :]
        normed, rstd = normed_rows(mixed_ref[rows_of(c), :])
        mixed_grad = cot + norm_back(gradient, normed, rstd, gain)
        grad_ref[rows_of(c), :] = mixed_grad
        all_ref[t, rows_of(c), :] = mixed_grad.astype(BF16)
        gather.start(c)
        terms = (mixed_grad, gradient * normed, gradient, cot)
        sums = [s + jnp.sum(v, axis=0, keepdims=True) for s, v in zip(sums, terms)]
    zero = jnp.zeros_like(gain)
    sums_ref[...] = jnp.concatenate([zero, zero] + sums + [zero, zero], axis=0)
    for c in range(feed.chunks):
        feed.middle(c)
    outer.middle()
    for c in range(gather.chunks):
        gather.forward(c)
    inner.middle()
    bias = vec_ref[5:6, :]
    for c in range(feed.chunks):
        out_ref[rows_of(c), :] = mixed_ref[rows_of(c), :] + feed.result(c) + bias
    gather.finish()
    wo_out_ref[...] = outer.result()
    wi_out_ref[...] = inner.result()
    first.finish()
    feed.finish()
    outer.finish()
    inner.finish()


def fourth_kernel(
    dp, part_ref, x_ref, mixed_grad_ref, vec_ref, sums_ref, wgrad_ref,
    input_grad_ref, wout_ref, vout_ref,
    near, total, far, r_send, r_recv,
    w_near, w_total, w_far, w0, w1, w2, w3, group, t_send, t_recv, whole, v_send, v_recv,
):
    d, t, sib, opp, diag = places()
    greet(dp, (sib, opp, diag))
    scat = Scatter(part_ref, near, total, far, r_send, r_recv)
    scat.start()

    weights = WeightScatter(dp, wgrad_ref, w_near, w_total, w_far, (w0, w1), (w2, w3))
    weights.start()
    for c in range(scat.chunks):
        scat.middle(c)
    weights.middle()
    gain = vec_ref[0:1, :]
    sums = [jnp.zeros_like(gain) for _ in range(2)]
    for c in range(scat.chunks):
        gradient = scat.result(c)
        normed, rstd = normed_rows(x_ref[rows_of(c), :])
        input_grad_ref[rows_of(c), :] = mixed_grad_ref[rows_of(c), :] + norm_back(
            gradient, normed, rstd, gain
        )
        terms = (gradient * normed, gradient)
        sums = [s + jnp.sum(v, axis=0, keepdims=True) for s, v in zip(sums, terms)]
    mine = sums_ref[...] + jnp.concatenate(
        sums + [jnp.zeros((VROWS - 2, gain.shape[1]), F32)], axis=0
    )
    group[t] = mine
    tensor_copies = [
        pltpu.make_async_remote_copy(
            src_ref=group.at[t],
            dst_ref=group.at[t],
            send_sem=t_send.at[i],
            recv_sem=t_recv.at[i],
            device_id=(d, peer),
            device_id_type=MESH,
        )
        for i, peer in enumerate((sib, opp, diag))
    ]
    for copy in tensor_copies:
        copy.start()
    for copy in tensor_copies:
        copy.wait()
    over_group = jnp.sum(group[...], axis=0)
    row = lax.broadcasted_iota(jnp.int32, mine.shape, 0)
    whole[d] = jnp.where(row < 6, over_group, mine)

    def vector_copy(k):
        return dp_copy(dp, k, whole.at[d], whole.at[d], v_send, v_recv)

    each_peer(dp, lambda k: vector_copy(k).start())
    wout_ref[...] = weights.result()
    each_peer(dp, lambda k: vector_copy(k).wait())
    vout_ref[...] = jnp.sum(whole[...], axis=0)
    scat.finish()
    weights.finish()


VM = pl.BlockSpec(memory_space=pltpu.VMEM)
ANY = pl.BlockSpec(memory_space=pl.ANY)


def comm_call(kernel, ident, in_specs, outs, out_specs, scratch, flops=20_000_000_000):
    return pl.pallas_call(
        kernel,
        out_shape=tuple(jax.ShapeDtypeStruct(s, dt) for s, dt in outs),
        in_specs=in_specs,
        out_specs=tuple(out_specs),
        scratch_shapes=scratch,
        cost_estimate=pl.CostEstimate(flops=flops, bytes_accessed=4_000_000, transcendentals=0),
        compiler_params=pltpu.CompilerParams(
            collective_id=ident, has_side_effects=True, vmem_limit_bytes=36 * 1024 * 1024
        ),
    )


def token_kernel(a_ref, b_ref, o_ref):
    o_ref[...] = lax.dot_general(
        a_ref[...], b_ref[...], (((0,), (0,)), ((), ())), preferred_element_type=F32
    ).astype(o_ref.dtype)


def token_product(left, right):
    tokens, m = left.shape
    n = right.shape[1]
    tile = 256
    return pl.pallas_call(
        token_kernel,
        grid=(m // tile,),
        out_shape=jax.ShapeDtypeStruct((m, n), BF16),
        in_specs=[
            pl.BlockSpec((tokens, tile), lambda i: (0, i)),
            pl.BlockSpec((tokens, n), lambda i: (0, 0)),
        ],
        out_specs=pl.BlockSpec((tile, n), lambda i: (i, 0)),
        cost_estimate=pl.CostEstimate(
            flops=2 * tokens * m * n, bytes_accessed=2 * (tokens * (m + n) + m * n), transcendentals=0
        ),
        compiler_params=pltpu.CompilerParams(vmem_limit_bytes=24 * 1024 * 1024),
    )(left, right)


def attend(operands):
    queries, key_rows, values = operands
    score_scale = 1.0 / math.sqrt(HD)
    scores = (
        jnp.einsum(
            "qhd,khd->hqk",
            split_heads(queries),
            split_heads(key_rows),
            preferred_element_type=jnp.float32,
        )
        * score_scale
    )
    row_max = jnp.max(scores, axis=-1, keepdims=True)
    log_total = row_max + jnp.log(jnp.sum(jnp.exp(scores - row_max), axis=-1, keepdims=True))
    prob_low = jnp.exp(scores - log_total).astype(jnp.bfloat16)
    context = jnp.einsum(
        "hqk,khd->qhd", prob_low, split_heads(values), preferred_element_type=jnp.float32
    )
    return (context.reshape(queries.shape).astype(jnp.bfloat16), log_total)


def attend_back_kernel(heads, qkv_ref, grad_ref, log_ref, out_ref, sums_ref, queries_t, keys, vals):
    scale = 1.0 / math.sqrt(HD)
    width = heads * HD
    frames = qkv_ref.shape[0]
    tile = 256
    for h in range(heads):
        lanes = slice(h * HD, (h + 1) * HD)
        key = qkv_ref[:, width + h * HD : width + (h + 1) * HD]
        value = qkv_ref[:, 2 * width + h * HD : 2 * width + (h + 1) * HD]
        key_t = key.astype(F32).T.astype(BF16)
        keys[...] = jnp.zeros_like(keys)
        vals[...] = jnp.zeros_like(vals)

        def step(i, carry, lanes=lanes, key=key, value=value, key_t=key_t, h=h):
            start = pl.multiple_of(i * tile, tile)
            at = pl.ds(start, tile)
            query = qkv_ref[at, lanes]
            grad = grad_ref[at, lanes]
            scores = matmul_nt(key, query) * scale
            prob = jnp.exp(scores - log_ref[h : h + 1, at])
            vals[...] += matmul(prob.astype(BF16), grad)
            prob_grad = matmul_nt(value, grad)
            row_dot = jnp.sum(prob * prob_grad, axis=0, keepdims=True)
            score_grad = (prob * (prob_grad - row_dot) * scale).astype(BF16)
            keys[...] += matmul(score_grad, query)
            queries_t[lanes, at] = matmul(key_t, score_grad)
            return carry

        lax.fori_loop(0, frames // tile, step, 0)
        value_grad = vals[...]
        out_ref[:, width + h * HD : width + (h + 1) * HD] = keys[...].astype(BF16)
        out_ref[:, 2 * width + h * HD : 2 * width + (h + 1) * HD] = value_grad.astype(BF16)
        query_grad = queries_t[lanes, :].T
        out_ref[:, lanes] = query_grad.astype(BF16)
        sums_ref[0:1, lanes] = jnp.sum(query_grad, axis=0, keepdims=True)
        sums_ref[1:2, lanes] = jnp.sum(value_grad, axis=0, keepdims=True)


def attend_back(qkv, context_grad, log_total):
    clips, frames, wide = qkv.shape
    width = context_grad.shape[2]
    heads = width // HD

    def spec(*shape):
        return pl.BlockSpec((None,) + shape, lambda c: (c, 0, 0))

    return pl.pallas_call(
        functools.partial(attend_back_kernel, heads),
        grid=(clips,),
        out_shape=(
            jax.ShapeDtypeStruct((clips, frames, wide), BF16),
            jax.ShapeDtypeStruct((clips, 2, width), F32),
        ),
        in_specs=[spec(frames, wide), spec(frames, width), spec(heads, frames)],
        out_specs=(spec(frames, wide), spec(2, width)),
        scratch_shapes=[
            pltpu.VMEM((width, frames), F32),
            pltpu.VMEM((frames, HD), F32),
            pltpu.VMEM((frames, HD), F32),
        ],
        cost_estimate=pl.CostEstimate(
            flops=10 * clips * heads * frames * frames * HD,
            bytes_accessed=6_000_000,
            transcendentals=clips * heads * frames * frames,
        ),
        compiler_params=pltpu.CompilerParams(vmem_limit_bytes=36 * 1024 * 1024),
    )(qkv, context_grad, log_total)


def on_device(
    dp,
    layer_input,
    out_cotangent,
    mix_gain,
    mix_shift,
    query_weight,
    query_bias,
    key_weight,
    value_weight,
    value_bias,
    output_weight,
    output_bias,
    feed_gain,
    feed_shift,
    inner_weight,
    inner_bias,
    outer_weight,
    outer_bias,
):
    d = lax.axis_index("dp")
    t = lax.axis_index("tensor")
    clips, share, feats = layer_input.shape
    rows = clips * share
    frames = share * 4
    width = query_weight.shape[1]
    shard = query_weight.shape[0]
    hidden_units = inner_weight.shape[1]

    def placed_bias(bias):
        full = jnp.zeros((HD, bias.shape[1]), F32)
        full = lax.dynamic_update_slice(full, bias.astype(F32), (d * bias.shape[0], 0))
        return full.T.reshape(-1)

    vectors = jnp.stack([mix_gain, mix_shift, output_bias, feed_gain, feed_shift, outer_bias])
    upper = lax.dynamic_update_slice(
        jnp.zeros((6, feats), F32), vectors.astype(F32), (0, d * vectors.shape[1])
    )
    none = jnp.zeros((width,), F32)
    head_row = jnp.concatenate([placed_bias(query_bias), none, placed_bias(value_bias), none])
    small = jnp.concatenate([upper, head_row[None], placed_bias(inner_bias)[None]], axis=0)
    pack = jnp.concatenate([query_weight, key_weight, value_weight, output_weight], axis=1)

    x = layer_input.reshape(rows, feats)
    cot = out_cotangent.reshape(rows, feats)
    block = (4, rows, feats)

    def to_tokens(gathered):
        return (
            gathered.reshape(4, clips, share, feats)
            .transpose(1, 0, 2, 3)
            .reshape(clips * frames, feats)
        )

    def to_blocks(tokens):
        return (
            tokens.astype(BF16)
            .reshape(clips, 4, share, feats)
            .transpose(1, 0, 2, 3)
            .reshape(block)
        )

    gathered_pack, inner_all, vec, low_one, cot_all = comm_call(
        functools.partial(first_kernel, dp),
        1,
        [VM, VM, VM, ANY, ANY],
        [((dp,) + pack.shape, BF16), ((dp,) + inner_weight.shape, BF16), ((VROWS, feats), F32), (block, BF16), (block, BF16)],
        [ANY, ANY, VM, VM, VM],
        [
            pltpu.VMEM((dp, VROWS, feats), F32),
            pltpu.SemaphoreType.DMA((dp,)),
            pltpu.SemaphoreType.DMA((dp,)),
            pltpu.SemaphoreType.DMA((2,)),
        ]
        + gather_scratch(rows)
        + gather_scratch(rows)
        + sem_pairs(dp)
        + sem_pairs(dp),
    )(x, cot, small, pack, inner_weight)
    inner_full = inner_all.reshape(feats, hidden_units)
    flat_one = to_tokens(low_one)
    cot_tokens = to_tokens(cot_all)
    attn_weights = gathered_pack.reshape(feats, 4 * width)
    qkv_full = attn_weights[:, : 3 * width]
    output_full = attn_weights[:, 3 * width :]
    qkv = (matmul(flat_one, qkv_full) + vec[6, : 3 * width]).astype(BF16)
    clip_qkv = qkv.reshape(clips, frames, 3 * width)
    clip_queries = clip_qkv[:, :, :width]
    clip_keys = clip_qkv[:, :, width : 2 * width]
    clip_values = clip_qkv[:, :, 2 * width :]
    context, log_total = lax.map(attend, (clip_queries, clip_keys, clip_values))
    flat_context = context.reshape(clips * frames, width)
    attn_part = to_blocks(matmul_nt(flat_context, output_full))

    mixed, low_two, outer_all = comm_call(
        functools.partial(second_kernel, dp),
        2,
        [VM, VM, VM, ANY],
        [((rows, feats), F32), (block, BF16), ((dp,) + outer_weight.shape, BF16)],
        [VM, VM, ANY],
        scatter_scratch(rows, feats)
        + gather_scratch(rows)
        + [pltpu.SemaphoreType.DMA]
        + sem_pairs(dp),
    )(attn_part, x, vec, outer_weight)
    outer_full = outer_all.reshape(feats, hidden_units)
    flat_two = to_tokens(low_two)
    preact = matmul(flat_two, inner_full) + vec[7, :hidden_units]
    hidden = gelu_value(preact).astype(BF16)
    preact_grad = matmul(cot_tokens, outer_full) * gelu_slope(preact)
    preact_low = preact_grad.astype(BF16)
    inner_bias_sum = jnp.sum(preact_grad, axis=0)
    norm_two_part = to_blocks(matmul_nt(preact_low, inner_full))
    feed_part = to_blocks(matmul_nt(hidden, outer_full))

    outer_part = token_product(cot_tokens, hidden)
    inner_part = token_product(flat_two, preact_low)
    by_shard = (dp, shard, hidden_units)

    (
        mixed_grad, mixed_all, layer_output, sums, outer_weight_grad, inner_weight_grad,
    ) = comm_call(
        functools.partial(third_kernel, dp),
        3,
        [VM] * 7,
        [
            ((rows, feats), F32),
            (block, BF16),
            ((rows, feats), F32),
            ((VROWS, feats), F32),
            ((shard, hidden_units), F32),
            ((shard, hidden_units), F32),
        ],
        [VM] * 6,
        scatter_scratch(rows, feats)
        + scatter_scratch(rows, feats)
        + gather_scratch(rows)
        + weight_scratch(dp, shard, hidden_units)
        + weight_scratch(dp, shard, hidden_units),
    )(
        norm_two_part, feed_part, mixed, cot, vec,
        outer_part.reshape(by_shard), inner_part.reshape(by_shard),
    )
    mixed_tokens = to_tokens(mixed_all)
    output_part = token_product(mixed_tokens, flat_context)
    context_grad = matmul(mixed_tokens, output_full).astype(BF16).reshape(clips, frames, width)
    low_grads, head_sums = attend_back(
        clip_qkv, context_grad, log_total.reshape(clips, width // HD, frames)
    )
    low_grads = low_grads.reshape(clips * frames, 3 * width)
    head_sums = jnp.sum(head_sums, axis=0)
    norm_one_part = to_blocks(matmul_nt(low_grads, qkv_full))
    attn_wpart = jnp.concatenate([token_product(flat_one, low_grads), output_part], axis=1)
    bias_row = jnp.concatenate(
        [head_sums[0], none, head_sums[1], none]
    )
    sums = sums + jnp.concatenate(
        [jnp.zeros((VROWS - 2, feats), F32), bias_row[None], inner_bias_sum[None]], axis=0
    )

    input_grad, attn_grads, vector_sums = comm_call(
        functools.partial(fourth_kernel, dp),
        4,
        [VM] * 6,
        [((rows, feats), F32), ((shard, 4 * width), F32), ((VROWS, feats), F32)],
        [VM] * 3,
        scatter_scratch(rows, feats)
        + weight_scratch(dp, shard, 4 * width)
        + [
            pltpu.VMEM((4, VROWS, feats), F32),
            pltpu.SemaphoreType.DMA((3,)),
            pltpu.SemaphoreType.DMA((3,)),
            pltpu.VMEM((dp, VROWS, feats), F32),
            pltpu.SemaphoreType.DMA((dp,)),
            pltpu.SemaphoreType.DMA((dp,)),
        ],
    )(norm_one_part, x, mixed_grad, vec, sums, attn_wpart.reshape(dp, shard, 4 * width))

    piece = feats // (4 * dp)
    mine = lax.dynamic_slice(vector_sums, (0, (d * 4 + t) * piece), (VROWS, piece))

    def bias_share(vector, like):
        table = vector.reshape(-1, HD).T
        return lax.dynamic_slice(table, (d * like.shape[0], 0), like.shape)

    return (
        layer_output.reshape(layer_input.shape),
        input_grad.reshape(layer_input.shape),
        mine[0],
        mine[1],
        attn_grads[:, :width],
        bias_share(vector_sums[6, :width], query_bias),
        attn_grads[:, width : 2 * width],
        attn_grads[:, 2 * width : 3 * width],
        bias_share(vector_sums[6, 2 * width : 3 * width], value_bias),
        attn_grads[:, 3 * width :],
        mine[2],
        mine[3],
        mine[4],
        inner_weight_grad,
        bias_share(vector_sums[7, :hidden_units], inner_bias),
        outer_weight_grad,
        mine[5],
    )


def solution(mesh):
    placed = (
        P("dp", "tensor", None),
        P("dp", "tensor", None),
        P("dp"),
        P("dp"),
        P("dp", "tensor"),
        P("dp", "tensor"),
        P("dp", "tensor"),
        P("dp", "tensor"),
        P("dp", "tensor"),
        P("dp", "tensor"),
        P("dp"),
        P("dp"),
        P("dp"),
        P("dp", "tensor"),
        P("dp", "tensor"),
        P("dp", "tensor"),
        P("dp"),
    )
    return jax.shard_map(
        functools.partial(on_device, mesh.shape["dp"]),
        mesh=mesh,
        in_specs=placed,
        out_specs=(
            P("dp", "tensor", None),
            P("dp", "tensor", None),
            P(("dp", "tensor")),
            P(("dp", "tensor")),
            P("dp", "tensor"),
            P("dp", "tensor"),
            P("dp", "tensor"),
            P("dp", "tensor"),
            P("dp", "tensor"),
            P("dp", "tensor"),
            P(("dp", "tensor")),
            P(("dp", "tensor")),
            P(("dp", "tensor")),
            P("dp", "tensor"),
            P("dp", "tensor"),
            P("dp", "tensor"),
            P(("dp", "tensor")),
        ),
        check_vma=False,
    )
```
